32 devices in a mesh: pole: 2 (over y), row: 4 (over z), col: 4 (over x, core).
Axes of the slice: x: 2, y: 2, z: 4, core: 2. Of those that a mesh axis runs over, the one named last changes fastest.
Arguments:
- root_inverse: float32 [16384, 8192], P(('pole', 'row'), 'col'), parts along dimension 0, may hold values from -6 to 6
- lower_one: float32 [16384, 512], P(('pole', 'row'), 'col'), parts along dimension 0, may hold values from -0.0625 to 0.0625
- pattern_one: int32 [64, 4], replicated, may hold values from 0 to 1, as said below
- diag_one: float32 [256, 512], P('pole', 'col'), parts along dimension 0, may hold values from -6 to 6
- lower_two: float32 [16384, 1024], P(('pole', 'row'), 'col'), parts along dimension 0, may hold values from -0.0625 to 0.0625
- pattern_two: int32 [64, 8], replicated, may hold values from 0 to 1, as said below
- parent_two: int32 [8], replicated, may hold values from 0 to 3, as said below
- lower_parent: float32 [256, 1024], P('pole', 'col'), parts along dimension 0, may hold values from -0.5 to 0.5
- diag_two: float32 [256, 1024], P('pole', 'col'), parts along dimension 0, may hold values from -6 to 6
Outputs:
- inverse_off_one: float32 [16384, 512], P(('pole', 'row'), 'col'), parts along dimension 0
- inverse_diagonal_first: float32 [256, 512], P('pole', 'col'), parts along dimension 0
- inverse_off_two: float32 [16384, 1024], P(('pole', 'row'), 'col'), parts along dimension 0
- inverse_parent_two: float32 [256, 1024], P('pole', 'col'), parts along dimension 0
- inverse_diag_two: float32 [256, 1024], P('pole', 'col'), parts along dimension 0
The draws below stay inside these ranges and needn't reach their ends.
There are 2 independent parts, one for each index of `pole`. The reference program is written for one: setup_inputs(seed, part) draws one part's arguments, and reference() takes and returns one part's arrays. A program takes and returns all parts, laid end to end along the dimension named above; an argument that names none is the same for every part. Nothing has to cross between parts.
Inputs may be any that keep to these rules, and one draw needn't show every extreme that they name: pattern_one[i, k] is 1 where root block row i lies in the structure of first-level supernode k. `parent_two`: each first-level supernode is the parent of exactly two second-level supernodes. pattern_two[i, m] is 1 only where pattern_one[i, parent_two[m]] is 1.
All inputs are finite; a program needn't handle non-finite values.
Results may differ from the reference program's by a relative error of at most 0.000088.
Values sent between devices are 32-bit elements; how exact they have to be, the bound alone decides.
A program may use at most 128 MiB of HBM per device.

```python
import jax
import jax.numpy as jnp
from jax import lax

BLOCK_SIDE = 128
ROOT_BLOCKS = 64
SUPERNODES_FIRST = 4
SUPER_TWO = 8
ROOT_ORDER = 8192
ORDER_ONE = 512
ORDER_TWO = 1024


def structure(key):
    level_key = jax.random.fold_in(key, 101)
    entry_key = jax.random.fold_in(key, 202)
    parent_key = jax.random.fold_in(key, 303)
    retain_key = jax.random.fold_in(key, 404)
    density = jax.random.randint(level_key, (ROOT_BLOCKS, 1), 0, 8)
    first = (jax.random.randint(entry_key, (ROOT_BLOCKS, SUPERNODES_FIRST), 0, 8) < density).astype(jnp.int32)
    pair_ids = jnp.arange(SUPERNODES_FIRST, dtype=jnp.int32)
    far_parent = (pair_ids + SUPERNODES_FIRST // 2) % SUPERNODES_FIRST
    drawn_parent = jax.random.permutation(parent_key, pair_ids).astype(jnp.int32)
    parents = jnp.stack([far_parent, drawn_parent], axis=1).reshape(SUPER_TWO).astype(jnp.int32)
    retained = jax.random.randint(retain_key, (ROOT_BLOCKS, SUPER_TWO), 0, 4) < 3
    second = jnp.where(retained, first[:, parents], 0).astype(jnp.int32)
    return (first, parents, second)


def draw_pattern_one(key, part):
    return structure(key)[0]


def draw_parent_two(key, part):
    return structure(key)[1]


def draw_pattern_two(key, part):
    return structure(key)[2]


def levels(own_key, shape, shards, low, high):
    factor_of = 1.0
    for position, parts in shards:
        heights = jax.random.uniform(jax.random.fold_in(jax.random.fold_in(own_key, 6), position), (parts,), jnp.float32, low / len(shards), high / len(shards))
        factor_of = factor_of * jnp.repeat(jnp.exp(heights), shape[position] // parts).reshape((-1,) + (1,) * (len(shape) - 1 - position))
    return factor_of


def bell_draw(key, shape, scale, bound, pieces=(), kind=jnp.bfloat16):
    factor_of = levels(key, shape, pieces, -0.22, 0.18) if pieces else 1.0
    values = jax.random.normal(key, shape, jnp.float32) * scale * factor_of
    return jnp.minimum(jnp.maximum(values, -bound), bound).astype(kind)


def setup_inputs(seed: int = 0, part: int = 0) -> dict:
    streams_of = jax.random.split(jax.random.key(seed), 10)
    part_keys = jax.random.split(jax.random.fold_in(streams_of[9], part), 10)
    root_inverse = bell_draw(part_keys[0], (ROOT_ORDER, ROOT_ORDER), 1.0, 6.0, ((0, 4), (1, 4)), jnp.float32)
    lower_one = bell_draw(part_keys[1], (ROOT_ORDER, ORDER_ONE), ROOT_ORDER ** -0.5, 0.0625, ((0, 4), (1, 4)), jnp.float32)
    pattern_one = draw_pattern_one(jax.random.fold_in(streams_of[9], 71), part)
    diag_one = bell_draw(part_keys[3], (BLOCK_SIDE, ORDER_ONE), 1.0, 6.0, ((1, 4),), jnp.float32)
    lower_two = bell_draw(part_keys[4], (ROOT_ORDER, ORDER_TWO), ROOT_ORDER ** -0.5, 0.0625, ((0, 4), (1, 4)), jnp.float32)
    pattern_two = draw_pattern_two(jax.random.fold_in(streams_of[9], 71), part)
    parent_two = draw_parent_two(jax.random.fold_in(streams_of[9], 71), part)
    lower_parent = bell_draw(part_keys[7], (BLOCK_SIDE, ORDER_TWO), BLOCK_SIDE ** -0.5, 0.5, ((1, 4),), jnp.float32)
    diag_two = bell_draw(part_keys[8], (BLOCK_SIDE, ORDER_TWO), 1.0, 6.0, ((1, 4),), jnp.float32)
    return dict(root_inverse=root_inverse, lower_one=lower_one, pattern_one=pattern_one, diag_one=diag_one, lower_two=lower_two, pattern_two=pattern_two, parent_two=parent_two, lower_parent=lower_parent, diag_two=diag_two)


PRECISION_MODE = lax.Precision.HIGHEST


def expand_blocks(pattern):
    count_rows, count_cols = pattern.shape
    spread = jnp.broadcast_to(pattern.astype(jnp.float32)[:, None, :, None], (count_rows, BLOCK_SIDE, count_cols, BLOCK_SIDE))
    return spread.reshape(count_rows * BLOCK_SIDE, count_cols * BLOCK_SIDE)


def block_inner(masked, solved):
    rows_here = masked.shape[0]
    blocks = masked.shape[1] // BLOCK_SIDE
    inner = jnp.einsum("ikb,ikc->bkc", masked.reshape(rows_here, blocks, BLOCK_SIDE), solved.reshape(rows_here, blocks, BLOCK_SIDE), precision=PRECISION_MODE)
    return inner.reshape(BLOCK_SIDE, blocks * BLOCK_SIDE)


def reference(root_inverse, lower_one, pattern_one, diag_one, lower_two, pattern_two, parent_two, lower_parent, diag_two):
    mask_one = expand_blocks(pattern_one)
    masked_one = lower_one * mask_one
    solved_one = jnp.dot(root_inverse, masked_one, precision=PRECISION_MODE, preferred_element_type=jnp.float32)
    inverse_off_one = -(mask_one * solved_one)
    inverse_diagonal_first = diag_one + block_inner(masked_one, solved_one)
    mask_two = expand_blocks(pattern_two)
    masked_two = lower_two * mask_two
    selection_matrix = (parent_two[None, :] == jnp.arange(SUPERNODES_FIRST, dtype=jnp.int32)[:, None]).astype(jnp.float32)
    parent_cols = jnp.einsum("ikb,km->imb", inverse_off_one.reshape(ROOT_ORDER, SUPERNODES_FIRST, BLOCK_SIDE), selection_matrix, precision=PRECISION_MODE)
    link = lower_parent.reshape(BLOCK_SIDE, SUPER_TWO, BLOCK_SIDE)
    solved_two = jnp.dot(root_inverse, masked_two, precision=PRECISION_MODE, preferred_element_type=jnp.float32)
    solved_two = solved_two + jnp.einsum("imb,bme->ime", parent_cols, link, precision=PRECISION_MODE).reshape(ROOT_ORDER, ORDER_TWO)
    parent_diagonal = jnp.einsum("vfl,fo->vol", inverse_diagonal_first.reshape(BLOCK_SIDE, SUPERNODES_FIRST, BLOCK_SIDE), selection_matrix, precision=PRECISION_MODE)
    across = jnp.einsum("imb,ime->bme", parent_cols, masked_two.reshape(ROOT_ORDER, SUPER_TWO, BLOCK_SIDE), precision=PRECISION_MODE)
    across = across + jnp.einsum("bmd,dme->bme", parent_diagonal, link, precision=PRECISION_MODE)
    inverse_diag_two = diag_two + block_inner(masked_two, solved_two)
    inverse_diag_two = inverse_diag_two + jnp.einsum("dmb,dme->bme", link, across, precision=PRECISION_MODE).reshape(BLOCK_SIDE, ORDER_TWO)
    return (inverse_off_one, inverse_diagonal_first, -(mask_two * solved_two), -across.reshape(BLOCK_SIDE, ORDER_TWO), inverse_diag_two)
```

```python
import functools

import jax
import jax.numpy as jnp
from jax import lax
from jax.experimental import pallas as pl
from jax.experimental.pallas import tpu as pltpu
from jax.sharding import PartitionSpec as P

BLOCK_SIDE = 128
MODE = lax.Precision.HIGH


def product(left_part, right_part):
    return jnp.dot(left_part, right_part, precision=MODE, preferred_element_type=jnp.float32)


def transposed_product(left_part, right_part):
    return lax.dot_general(
        left_part,
        right_part,
        (((0,), (0,)), ((), ())),
        precision=MODE,
        preferred_element_type=jnp.float32,
    )


def pack_kernel(count, blocks_one, blocks_two, order_ref, one_ref, two_ref, out_ref, sem):
    blocks = blocks_one + blocks_two

    @pl.loop(0, count)
    def _(slot):
        tile = order_ref[slot]
        row = lax.div(tile, blocks) * BLOCK_SIDE
        block = lax.rem(tile, blocks)
        rows = pl.ds(pl.multiple_of(row, BLOCK_SIDE), BLOCK_SIDE)

        @pl.when(block < blocks_one)
        def _():
            cols = pl.ds(pl.multiple_of(block * BLOCK_SIDE, BLOCK_SIDE), BLOCK_SIDE)
            pltpu.make_async_copy(one_ref.at[rows, cols], out_ref.at[slot], sem).start()

        @pl.when(block >= blocks_one)
        def _():
            cols = pl.ds(
                pl.multiple_of((block - blocks_one) * BLOCK_SIDE, BLOCK_SIDE), BLOCK_SIDE
            )
            pltpu.make_async_copy(two_ref.at[rows, cols], out_ref.at[slot], sem).start()

    pltpu.make_async_copy(out_ref, out_ref, sem).wait()


def pack_pair(order, one, two):
    count = order.shape[0]
    return pl.pallas_call(
        functools.partial(
            pack_kernel, count, one.shape[1] // BLOCK_SIDE, two.shape[1] // BLOCK_SIDE
        ),
        out_shape=jax.ShapeDtypeStruct((count, BLOCK_SIDE, BLOCK_SIDE), jnp.float32),
        in_specs=[
            pl.BlockSpec(memory_space=pltpu.SMEM),
            pl.BlockSpec(memory_space=pl.ANY),
            pl.BlockSpec(memory_space=pl.ANY),
        ],
        out_specs=pl.BlockSpec(memory_space=pl.ANY),
        scratch_shapes=[pltpu.SemaphoreType.DMA],
        name="pack_pair",
    )(order, one, two)


def pick_kernel(count, blocks, order_ref, dense_ref, out_ref, sem):
    @pl.loop(0, count)
    def _(slot):
        tile = order_ref[slot]
        rows = pl.ds(
            pl.multiple_of(lax.div(tile, blocks) * BLOCK_SIDE, BLOCK_SIDE), BLOCK_SIDE
        )
        cols = pl.ds(
            pl.multiple_of(lax.rem(tile, blocks) * BLOCK_SIDE, BLOCK_SIDE), BLOCK_SIDE
        )
        pltpu.make_async_copy(dense_ref.at[rows, cols], out_ref.at[slot], sem).start()

    pltpu.make_async_copy(out_ref, out_ref, sem).wait()


def pick_tiles(order, dense):
    count = order.shape[0]
    return pl.pallas_call(
        functools.partial(pick_kernel, count, dense.shape[1] // BLOCK_SIDE),
        out_shape=jax.ShapeDtypeStruct((count, BLOCK_SIDE, BLOCK_SIDE), jnp.float32),
        in_specs=[
            pl.BlockSpec(memory_space=pltpu.SMEM),
            pl.BlockSpec(memory_space=pl.ANY),
        ],
        out_specs=pl.BlockSpec(memory_space=pl.ANY),
        scratch_shapes=[pltpu.SemaphoreType.DMA],
        name="pick_tiles",
    )(order, dense)


def spread_kernel(count, blocks, place_ref, packed_ref, out_ref, zeros, sem):
    zeros[...] = jnp.zeros_like(zeros)

    @pl.loop(0, count)
    def _(tile):
        place = place_ref[tile]
        rows = pl.ds(
            pl.multiple_of(lax.div(tile, blocks) * BLOCK_SIDE, BLOCK_SIDE), BLOCK_SIDE
        )
        cols = pl.ds(
            pl.multiple_of(lax.rem(tile, blocks) * BLOCK_SIDE, BLOCK_SIDE), BLOCK_SIDE
        )

        @pl.when(place >= 0)
        def _():
            pltpu.make_async_copy(packed_ref.at[place], out_ref.at[rows, cols], sem).start()

        @pl.when(place < 0)
        def _():
            pltpu.make_async_copy(zeros, out_ref.at[rows, cols], sem).start()

    pltpu.make_async_copy(out_ref, out_ref, sem).wait()


def spread_tiles(place, packed, blocks):
    count = place.shape[0]
    return pl.pallas_call(
        functools.partial(spread_kernel, count, blocks),
        out_shape=jax.ShapeDtypeStruct(
            (count // blocks * BLOCK_SIDE, blocks * BLOCK_SIDE), jnp.float32
        ),
        in_specs=[
            pl.BlockSpec(memory_space=pltpu.SMEM),
            pl.BlockSpec(memory_space=pl.ANY),
        ],
        out_specs=pl.BlockSpec(memory_space=pl.ANY),
        scratch_shapes=[
            pltpu.VMEM((BLOCK_SIDE, BLOCK_SIDE), jnp.float32),
            pltpu.SemaphoreType.DMA,
        ],
        name="spread_tiles",
    )(place, packed)


def expand_blocks(pattern):
    count_rows, count_cols = pattern.shape
    spread = jnp.broadcast_to(
        pattern.astype(jnp.float32)[:, None, :, None],
        (count_rows, BLOCK_SIDE, count_cols, BLOCK_SIDE),
    )
    return spread.reshape(count_rows * BLOCK_SIDE, count_cols * BLOCK_SIDE)


def gather_plane(packed):
    ranks_col = lax.axis_size("col")
    whole = lax.all_gather(packed, "row", axis=0)
    swapped = lax.all_to_all(whole, "col", split_axis=0, concat_axis=0, tiled=True)
    return swapped.reshape((ranks_col, -1) + packed.shape)


def capacity_levels(total):
    if total < 16:
        return (total,)
    return tuple(sorted({-(-total * part // 24) for part in (10, 11, 12, 13, 14, 16, 24)}))


def with_capacity(
    capacity,
    tables,
    root_inverse,
    lower_one,
    diag_one,
    lower_two,
    parent_two,
    lower_parent,
    diag_two,
):
    order, rank, pattern = tables
    ranks_row, ranks_col, total = order.shape
    row, col = lax.axis_index("row"), lax.axis_index("col")
    rows_here, cols_here = root_inverse.shape
    row_blocks = rows_here // BLOCK_SIDE
    col_one, col_two = (
        lower_one.shape[1] // BLOCK_SIDE,
        lower_two.shape[1] // BLOCK_SIDE,
    )
    blocks = col_one + col_two
    share = ranks_row // ranks_col

    own = lax.dynamic_index_in_dim(
        lax.dynamic_index_in_dim(order, row, 0, False), col, 0, False
    )[:capacity]
    packed = pack_pair(own, lower_one, lower_two)
    plane = gather_plane(packed)

    here = lax.dynamic_slice_in_dim(rank, col * share, share, 0)
    base = (
        jnp.arange(ranks_col)[None, :, None] * share + jnp.arange(share)[:, None, None]
    ) * capacity
    place = jnp.where(here >= 0, here + base, -1).reshape(share, ranks_col, row_blocks, blocks)
    place = place.transpose(0, 2, 1, 3).reshape(-1)
    right = spread_tiles(
        place.astype(jnp.int32),
        plane.reshape(-1, BLOCK_SIDE, BLOCK_SIDE),
        ranks_col * blocks,
    )
    partial_sum = product(root_inverse, right)

    outs = lax.dynamic_index_in_dim(order, row, 0, False)[:, :capacity]
    tiles = (
        lax.div(outs, blocks) * (ranks_col * blocks)
        + jnp.arange(ranks_col, dtype=jnp.int32)[:, None] * blocks
        + lax.rem(outs, blocks)
    )
    chosen = pick_tiles(tiles.reshape(-1), partial_sum)
    summed = lax.psum_scatter(chosen, "col", scatter_dimension=0, tiled=True)

    own_rank = lax.dynamic_index_in_dim(
        lax.dynamic_index_in_dim(rank, row, 0, False), col, 0, False
    )
    own_rank = own_rank.reshape(row_blocks, blocks)
    solved_one = spread_tiles(own_rank[:, :col_one].reshape(-1), summed, col_one)
    direct = spread_tiles(own_rank[:, col_one:].reshape(-1), summed, col_two)

    own_pattern = lax.dynamic_index_in_dim(
        lax.dynamic_index_in_dim(pattern, row, 0, False), col, 0, False
    ).reshape(row_blocks, blocks)
    mask_one = expand_blocks(own_pattern[:, :col_one])
    mask_two = expand_blocks(own_pattern[:, col_one:])
    masked_one = lower_one * mask_one
    masked_two = lower_two * mask_two

    def part(array, index):
        return lax.slice_in_dim(array, index * BLOCK_SIDE, (index + 1) * BLOCK_SIDE, axis=1)

    inverse_off_one = -solved_one
    columns = lax.all_gather(inverse_off_one, "col", axis=1, tiled=True)
    inner_one = jnp.concatenate(
        [transposed_product(part(masked_one, k), part(solved_one, k)) for k in range(col_one)],
        axis=1,
    )
    inverse_diagonal_first = diag_one + lax.psum(inner_one, "row")
    diagonals = lax.all_gather(inverse_diagonal_first, "col", axis=1, tiled=True)

    owned_parent = lax.dynamic_slice_in_dim(parent_two, col * col_two, col_two, 0)
    solved, inner_two, across_part, parent_diagonals = [], [], [], []
    for m in range(col_two):
        start = owned_parent[m] * BLOCK_SIDE
        parent_cols = lax.dynamic_slice_in_dim(columns, start, BLOCK_SIDE, 1)
        parent_diagonals.append(lax.dynamic_slice_in_dim(diagonals, start, BLOCK_SIDE, 1))
        solved_m = part(direct, m) + product(parent_cols, part(lower_parent, m))
        solved.append(solved_m)
        inner_two.append(transposed_product(part(masked_two, m), solved_m))
        across_part.append(transposed_product(parent_cols, part(masked_two, m)))
    totals = lax.psum(jnp.concatenate(inner_two + across_part, axis=1), "row")
    across, diag = [], []
    for m in range(col_two):
        link = part(lower_parent, m)
        across_m = part(totals, col_two + m) + product(parent_diagonals[m], link)
        across.append(across_m)
        diag.append(part(diag_two, m) + part(totals, m) + transposed_product(link, across_m))
    return (
        inverse_off_one,
        inverse_diagonal_first,
        -(mask_two * jnp.concatenate(solved, axis=1)),
        -jnp.concatenate(across, axis=1),
        jnp.concatenate(diag, axis=1),
    )


def local(
    root_inverse,
    lower_one,
    pattern_one,
    diag_one,
    lower_two,
    pattern_two,
    parent_two,
    lower_parent,
    diag_two,
):
    ranks_row, ranks_col = lax.axis_size("row"), lax.axis_size("col")
    row_blocks = root_inverse.shape[0] // BLOCK_SIDE
    pattern = jnp.concatenate(
        [
            pattern_one.reshape(ranks_row, row_blocks, ranks_col, -1),
            pattern_two.reshape(ranks_row, row_blocks, ranks_col, -1),
        ],
        axis=3,
    )
    pattern = pattern.transpose(0, 2, 1, 3).reshape(ranks_row, ranks_col, -1).astype(jnp.int32)
    total = pattern.shape[2]
    running = jnp.cumsum(pattern, axis=2)
    counts = running[:, :, -1:]
    rank = jnp.where(pattern > 0, running - 1, -1)
    slot = jnp.where(pattern > 0, running - 1, counts + jnp.arange(total) - running)
    order = jnp.sum(
        jnp.where(
            slot[:, :, None, :] == jnp.arange(total)[:, None],
            jnp.arange(total, dtype=jnp.int32),
            0,
        ),
        axis=3,
        dtype=jnp.int32,
    )
    levels = capacity_levels(total)
    operands = (
        (order, rank.astype(jnp.int32), pattern),
        root_inverse,
        lower_one,
        diag_one,
        lower_two,
        parent_two,
        lower_parent,
        diag_two,
    )
    branches = [functools.partial(with_capacity, level) for level in levels]
    if len(branches) == 1:
        return branches[0](*operands)
    index = jnp.sum(jnp.max(counts) > jnp.array(levels[:-1])).astype(jnp.int32)
    return lax.switch(index, branches, *operands)


def solution(mesh):
    return jax.shard_map(
        local,
        mesh=mesh,
        in_specs=(
            P(("pole", "row"), "col"),
            P(("pole", "row"), "col"),
            P(),
            P("pole", "col"),
            P(("pole", "row"), "col"),
            P(),
            P(),
            P("pole", "col"),
            P("pole", "col"),
        ),
        out_specs=(
            P(("pole", "row"), "col"),
            P("pole", "col"),
            P(("pole", "row"), "col"),
            P("pole", "col"),
            P("pole", "col"),
        ),
        check_vma=False,
    )
```

```python
import functools

import jax
import jax.numpy as jnp
from jax import lax
from jax.experimental import pallas as pl
from jax.experimental.pallas import tpu as pltpu
from jax.sharding import PartitionSpec as P

BLOCK_SIDE = 128
MODE = lax.Precision.HIGH
MESH = pl.DeviceIdType.MESH
VMEM_LIMIT = 58 * 1024 * 1024
SMEM_SPEC = pl.BlockSpec(memory_space=pltpu.SMEM)
VMEM_SPEC = pl.BlockSpec(memory_space=pltpu.VMEM)


def product(left_part, right_part):
    return jnp.dot(left_part, right_part, precision=MODE, preferred_element_type=jnp.float32)


def transposed_product(left_part, right_part):
    return lax.dot_general(
        left_part,
        right_part,
        (((0,), (0,)), ((), ())),
        precision=MODE,
        preferred_element_type=jnp.float32,
    )


def halves(value):
    high = value.astype(jnp.bfloat16)
    return high, (value - high.astype(jnp.float32)).astype(jnp.bfloat16)


def dot_f32(left, right, dims):
    left_high, left_low = halves(left)
    right_high, right_low = halves(right)
    dot = functools.partial(
        lax.dot_general,
        dimension_numbers=(dims, ((), ())),
        preferred_element_type=jnp.float32,
    )
    return dot(left_high, right_high) + (dot(left_high, right_low) + dot(left_low, right_high))


PLAIN = ((1,), (0,))
TRANSPOSED = ((0,), (0,))


def block_at(index):
    return pl.ds(pl.multiple_of(index * BLOCK_SIDE, BLOCK_SIDE), BLOCK_SIDE)


def pack_kernel(count, blocks_one, blocks_two, order_ref, one_ref, two_ref, out_ref):
    blocks = blocks_one + blocks_two

    @pl.loop(0, count)
    def _(slot):
        tile = order_ref[slot]
        rows = block_at(lax.div(tile, blocks))
        block = lax.rem(tile, blocks)

        @pl.when(block < blocks_one)
        def _():
            out_ref[slot] = one_ref[rows, block_at(block)]

        @pl.when(block >= blocks_one)
        def _():
            out_ref[slot] = two_ref[rows, block_at(block - blocks_one)]


def pack_pair(order, one, two):
    count = order.shape[0]
    return pl.pallas_call(
        functools.partial(
            pack_kernel, count, one.shape[1] // BLOCK_SIDE, two.shape[1] // BLOCK_SIDE
        ),
        out_shape=jax.ShapeDtypeStruct((count, BLOCK_SIDE, BLOCK_SIDE), jnp.float32),
        in_specs=[SMEM_SPEC, VMEM_SPEC, VMEM_SPEC],
        out_specs=VMEM_SPEC,
        compiler_params=pltpu.CompilerParams(vmem_limit_bytes=VMEM_LIMIT),
        name="pack_pair",
    )(order, one, two)


def gather_kernel(ranks_row, ranks_col, share, cuts, own_ref, plane_ref, held, *sems):
    up_send, up_recv, down_send, down_recv, side_send, side_recv, local_sem = sems
    row, col = lax.axis_index("row"), lax.axis_index("col")

    barrier = pltpu.get_barrier_semaphore()

    def greet(axes):
        pl.semaphore_signal(barrier, inc=1, device_id=axes, device_id_type=MESH)

    @pl.when(row > 0)
    def _():
        greet({"row": row - 1})

    @pl.when(row < ranks_row - 1)
    def _():
        greet({"row": row + 1})

    for step in range(1, ranks_col):
        greet({"col": lax.rem(col + step, ranks_col)})
    friends = (
        (row > 0).astype(jnp.int32) + (row < ranks_row - 1).astype(jnp.int32) + ranks_col - 1
    )
    pl.semaphore_wait(barrier, friends)

    def upward(block, piece, source):
        return pltpu.make_async_remote_copy(
            src_ref=source,
            dst_ref=held.at[block, cuts[piece]],
            send_sem=up_send.at[block, piece],
            recv_sem=up_recv.at[block, piece],
            device_id={"row": row + 1},
            device_id_type=MESH,
        )

    def downward(block, piece, source):
        return pltpu.make_async_remote_copy(
            src_ref=source,
            dst_ref=held.at[block, cuts[piece]],
            send_sem=down_send.at[block, piece],
            recv_sem=down_recv.at[block, piece],
            device_id={"row": row - 1},
            device_id_type=MESH,
        )

    def sideways(block, piece, source):
        part = lax.rem(block, share)
        return pltpu.make_async_remote_copy(
            src_ref=source,
            dst_ref=plane_ref.at[col, part, cuts[piece]],
            send_sem=side_send.at[block, piece],
            recv_sem=side_recv.at[col, part, piece],
            device_id={"col": lax.div(block, share)},
            device_id_type=MESH,
        )

    def inward(block, piece, source):
        part = lax.rem(block, share)
        return pltpu.make_async_copy(
            source, plane_ref.at[col, part, cuts[piece]], local_sem.at[part, piece]
        )

    def deliver(block, piece, source):
        @pl.when(lax.div(block, share) != col)
        def _():
            sideways(block, piece, source).start()

        @pl.when(lax.div(block, share) == col)
        def _():
            inward(block, piece, source).start()

    pieces = range(len(cuts))
    for piece in pieces:
        source = own_ref.at[cuts[piece]]

        @pl.when(row < ranks_row - 1)
        def _():
            upward(row, piece, source).start()

        @pl.when(row > 0)
        def _():
            downward(row, piece, source).start()

        deliver(row, piece, source)

    @pl.loop(1, ranks_row)
    def _(step):
        for piece in pieces:
            below, above = row - step, row + step

            @pl.when(below >= 0)
            def _():
                source = held.at[below, cuts[piece]]
                upward(below, piece, source).wait_recv()

                @pl.when(row < ranks_row - 1)
                def _():
                    upward(below, piece, source).start()

                deliver(below, piece, source)

            @pl.when(above < ranks_row)
            def _():
                source = held.at[above, cuts[piece]]
                downward(above, piece, source).wait_recv()

                @pl.when(row > 0)
                def _():
                    downward(above, piece, source).start()

                deliver(above, piece, source)

    @pl.loop(0, ranks_row)
    def _(block):
        for piece in pieces:
            source = own_ref.at[cuts[piece]]

            @pl.when(jnp.logical_and(block <= row, row < ranks_row - 1))
            def _():
                upward(block, piece, source).wait_send()

            @pl.when(jnp.logical_and(block >= row, row > 0))
            def _():
                downward(block, piece, source).wait_send()

            @pl.when(lax.div(block, share) != col)
            def _():
                sideways(block, piece, source).wait_send()

            @pl.when(lax.div(block, share) == col)
            def _():
                inward(block, piece, source).wait()

    @pl.loop(0, share)
    def _(part):
        for piece in pieces:
            source = own_ref.at[cuts[piece]]
            for step in range(1, ranks_col):
                other = lax.rem(col + step, ranks_col)
                pltpu.make_async_remote_copy(
                    src_ref=source,
                    dst_ref=plane_ref.at[other, part, cuts[piece]],
                    send_sem=side_send.at[0, piece],
                    recv_sem=side_recv.at[other, part, piece],
                    device_id={"col": other},
                    device_id_type=MESH,
                ).wait_recv()


def gather_plane(packed, collective):
    ranks_row, ranks_col = lax.axis_size("row"), lax.axis_size("col")
    share = ranks_row // ranks_col
    count = packed.shape[0]
    pieces = min(4, count)
    edges = [count * piece // pieces for piece in range(pieces + 1)]
    cuts = [pl.ds(low, high - low) for low, high in zip(edges[:-1], edges[1:])]
    by_row = pltpu.SemaphoreType.DMA((ranks_row, pieces))
    return pl.pallas_call(
        functools.partial(gather_kernel, ranks_row, ranks_col, share, cuts),
        out_shape=jax.ShapeDtypeStruct((ranks_col, share) + packed.shape, packed.dtype),
        in_specs=[VMEM_SPEC],
        out_specs=VMEM_SPEC,
        scratch_shapes=[
            pltpu.VMEM((ranks_row,) + packed.shape, packed.dtype),
            by_row,
            by_row,
            by_row,
            by_row,
            by_row,
            pltpu.SemaphoreType.DMA((ranks_col, share, pieces)),
            pltpu.SemaphoreType.DMA((share, pieces)),
        ],
        compiler_params=pltpu.CompilerParams(
            collective_id=collective, has_side_effects=True, vmem_limit_bytes=VMEM_LIMIT
        ),
        name="gather_plane",
    )(packed)


def multiply_kernel(
    row_blocks,
    col_blocks,
    columns,
    tiles,
    place_ref,
    slot_ref,
    left_ref,
    plane_ref,
    out_ref,
    split,
    inner_list,
    inner_place,
    outer_list,
):
    split[tiles] = jnp.zeros_like(split[tiles])

    @pl.loop(0, tiles)
    def _(tile):
        high, low = halves(plane_ref[tile])
        split[tile] = jnp.concatenate([high, low], axis=1)

    @pl.loop(0, columns)
    def _(column):
        def scan_inner(block, found):
            place = place_ref[block * columns + column]

            @pl.when(place >= 0)
            def _():
                inner_list[found] = block
                inner_place[found] = place

            return found + (place >= 0).astype(jnp.int32)

        inner = lax.fori_loop(0, col_blocks, scan_inner, jnp.int32(0))
        inner_list[inner] = 0
        inner_place[inner] = tiles

        def scan_outer(block, found):
            kept = slot_ref[block * columns + column] >= 0

            @pl.when(kept)
            def _():
                outer_list[found] = block

            return found + kept.astype(jnp.int32)

        outer = lax.fori_loop(0, row_blocks, scan_outer, jnp.int32(0))

        @pl.loop(0, lax.div(outer + 1, 2))
        def _(pair):
            first = outer_list[2 * pair]
            second = outer_list[jnp.minimum(2 * pair + 1, outer - 1)]

            def step(index, total):
                a, b = inner_list[2 * index], inner_list[2 * index + 1]
                left = jnp.concatenate(
                    [
                        jnp.concatenate(
                            [left_ref[block_at(i), block_at(a)], left_ref[block_at(i), block_at(b)]],
                            axis=1,
                        )
                        for i in (first, second)
                    ],
                    axis=0,
                )
                high, low = halves(left)
                right = jnp.concatenate(
                    [split[inner_place[2 * index]], split[inner_place[2 * index + 1]]], axis=0
                )
                wide = jnp.dot(high, right, preferred_element_type=jnp.float32)
                narrow = jnp.dot(low, right[:, :BLOCK_SIDE], preferred_element_type=jnp.float32)
                return total + (wide[:, :BLOCK_SIDE] + (wide[:, BLOCK_SIDE:] + narrow))

            total = lax.fori_loop(
                0,
                lax.div(inner + 1, 2),
                step,
                jnp.zeros((2 * BLOCK_SIDE, BLOCK_SIDE), jnp.float32),
            )
            out_ref[slot_ref[first * columns + column]] = total[:BLOCK_SIDE]
            out_ref[slot_ref[second * columns + column]] = jnp.where(
                second == first, total[:BLOCK_SIDE], total[BLOCK_SIDE:]
            )


def multiply_tiles(place, slot, left, plane, count):
    col_blocks, columns = place.shape
    row_blocks = slot.shape[0]
    tiles = plane.shape[0]
    return pl.pallas_call(
        functools.partial(multiply_kernel, row_blocks, col_blocks, columns, tiles),
        out_shape=jax.ShapeDtypeStruct((count, BLOCK_SIDE, BLOCK_SIDE), jnp.float32),
        in_specs=[SMEM_SPEC, SMEM_SPEC, VMEM_SPEC, VMEM_SPEC],
        out_specs=VMEM_SPEC,
        scratch_shapes=[
            pltpu.VMEM((tiles + 1, BLOCK_SIDE, 2 * BLOCK_SIDE), jnp.bfloat16),
            pltpu.SMEM((col_blocks + 2,), jnp.int32),
            pltpu.SMEM((col_blocks + 2,), jnp.int32),
            pltpu.SMEM((row_blocks + 2,), jnp.int32),
        ],
        compiler_params=pltpu.CompilerParams(vmem_limit_bytes=VMEM_LIMIT),
        name="multiply_tiles",
    )(place.reshape(-1), slot.reshape(-1), left, plane)


def first_kernel(row_blocks, blocks_one, blocks, rank_ref, packed_ref, one_ref, off_ref, inner_ref):
    inner_ref[...] = jnp.zeros_like(inner_ref)

    @pl.loop(0, row_blocks)
    def _(block):
        for k in range(blocks_one):
            rank = rank_ref[block * blocks + k]
            cols = pl.ds(k * BLOCK_SIDE, BLOCK_SIDE)

            @pl.when(rank >= 0)
            def _():
                solved = packed_ref[rank]
                off_ref[block_at(block), cols] = -solved
                inner_ref[:, cols] += dot_f32(one_ref[block_at(block), cols], solved, TRANSPOSED)

            @pl.when(rank < 0)
            def _():
                off_ref[block_at(block), cols] = jnp.zeros((BLOCK_SIDE, BLOCK_SIDE), jnp.float32)


def first_level(rank, packed, one):
    row_blocks, blocks = rank.shape
    blocks_one = one.shape[1] // BLOCK_SIDE
    return pl.pallas_call(
        functools.partial(first_kernel, row_blocks, blocks_one, blocks),
        out_shape=(
            jax.ShapeDtypeStruct(one.shape, jnp.float32),
            jax.ShapeDtypeStruct((BLOCK_SIDE, one.shape[1]), jnp.float32),
        ),
        in_specs=[SMEM_SPEC, VMEM_SPEC, VMEM_SPEC],
        out_specs=(VMEM_SPEC, VMEM_SPEC),
        compiler_params=pltpu.CompilerParams(vmem_limit_bytes=VMEM_LIMIT),
        name="first_level",
    )(rank.reshape(-1), packed, one)


def second_kernel(
    row_blocks,
    blocks_one,
    blocks,
    rank_ref,
    parent_ref,
    packed_ref,
    two_ref,
    columns_ref,
    link_ref,
    off_ref,
    sums_ref,
):
    blocks_two = blocks - blocks_one
    sums_ref[...] = jnp.zeros_like(sums_ref)

    @pl.loop(0, row_blocks)
    def _(block):
        for m in range(blocks_two):
            rank = rank_ref[block * blocks + blocks_one + m]
            rows, cols = block_at(block), pl.ds(m * BLOCK_SIDE, BLOCK_SIDE)

            @pl.when(rank >= 0)
            def _():
                parent = columns_ref[rows, block_at(parent_ref[m])]
                masked = two_ref[rows, cols]
                solved = packed_ref[rank] + dot_f32(parent, link_ref[:, cols], PLAIN)
                off_ref[rows, cols] = -solved
                sums_ref[:, cols] += dot_f32(masked, solved, TRANSPOSED)
                sums_ref[:, pl.ds((blocks_two + m) * BLOCK_SIDE, BLOCK_SIDE)] += dot_f32(
                    parent, masked, TRANSPOSED
                )

            @pl.when(rank < 0)
            def _():
                off_ref[rows, cols] = jnp.zeros((BLOCK_SIDE, BLOCK_SIDE), jnp.float32)


def second_level(rank, parents, packed, two, columns, link):
    row_blocks, blocks = rank.shape
    blocks_two = two.shape[1] // BLOCK_SIDE
    return pl.pallas_call(
        functools.partial(second_kernel, row_blocks, blocks - blocks_two, blocks),
        out_shape=(
            jax.ShapeDtypeStruct(two.shape, jnp.float32),
            jax.ShapeDtypeStruct((BLOCK_SIDE, 2 * two.shape[1]), jnp.float32),
        ),
        in_specs=[SMEM_SPEC, SMEM_SPEC, VMEM_SPEC, VMEM_SPEC, VMEM_SPEC, VMEM_SPEC],
        out_specs=(VMEM_SPEC, VMEM_SPEC),
        compiler_params=pltpu.CompilerParams(vmem_limit_bytes=VMEM_LIMIT),
        name="second_level",
    )(rank.reshape(-1), parents, packed, two, columns, link)


def capacity_levels(total):
    if total < 16:
        return (total,)
    return tuple(sorted({-(-total * part // 24) for part in (11, 12, 13, 14, 24)}))


def with_capacity(
    collective,
    capacity,
    tables,
    root_inverse,
    lower_one,
    diag_one,
    lower_two,
    parent_two,
    lower_parent,
    diag_two,
):
    order, rank = tables
    ranks_row, ranks_col, total = order.shape
    row, col = lax.axis_index("row"), lax.axis_index("col")
    rows_here, cols_here = root_inverse.shape
    row_blocks = rows_here // BLOCK_SIDE
    col_one, col_two = (
        lower_one.shape[1] // BLOCK_SIDE,
        lower_two.shape[1] // BLOCK_SIDE,
    )
    blocks = col_one + col_two
    share = ranks_row // ranks_col

    own = lax.dynamic_index_in_dim(
        lax.dynamic_index_in_dim(order, row, 0, False), col, 0, False
    )[:capacity]
    plane = gather_plane(pack_pair(own, lower_one, lower_two), collective)

    here = lax.dynamic_slice_in_dim(rank, col * share, share, 0)
    base = (
        jnp.arange(ranks_col, dtype=jnp.int32)[None, :, None] * share
        + jnp.arange(share, dtype=jnp.int32)[:, None, None]
    ) * capacity
    place = jnp.where(here >= 0, here + base, -1).reshape(share, ranks_col, row_blocks, blocks)
    place = place.transpose(0, 2, 1, 3).reshape(share * row_blocks, ranks_col * blocks)
    mine = lax.dynamic_index_in_dim(rank, row, 0, False)
    start = jnp.arange(ranks_col, dtype=jnp.int32)[:, None] * capacity
    slot = jnp.where(mine >= 0, mine + start, -1).reshape(ranks_col, row_blocks, blocks)
    slot = slot.transpose(1, 0, 2).reshape(row_blocks, ranks_col * blocks)
    partial_sum = multiply_tiles(
        place,
        slot,
        root_inverse,
        plane.reshape(-1, BLOCK_SIDE, BLOCK_SIDE),
        ranks_col * capacity,
    )
    summed = lax.psum_scatter(partial_sum, "col", scatter_dimension=0, tiled=True)

    own_rank = lax.dynamic_index_in_dim(mine, col, 0, False).reshape(row_blocks, blocks)
    inverse_off_one, inner_one = first_level(own_rank, summed, lower_one)
    columns = lax.all_gather(inverse_off_one, "col", axis=1, tiled=True)
    inverse_diagonal_first = diag_one + lax.psum(inner_one, "row")
    diagonals = lax.all_gather(inverse_diagonal_first, "col", axis=1, tiled=True)

    parents = lax.dynamic_slice_in_dim(parent_two, col * col_two, col_two, 0)
    inverse_off_two, sums = second_level(
        own_rank, parents, summed, lower_two, columns, lower_parent
    )
    totals = lax.psum(sums, "row")

    def part(array, index):
        return lax.slice_in_dim(array, index * BLOCK_SIDE, (index + 1) * BLOCK_SIDE, axis=1)

    across, diag = [], []
    for m in range(col_two):
        link = part(lower_parent, m)
        parent_diagonal = lax.dynamic_slice_in_dim(
            diagonals, parents[m] * BLOCK_SIDE, BLOCK_SIDE, 1
        )
        across_m = part(totals, col_two + m) + product(parent_diagonal, link)
        across.append(across_m)
        diag.append(part(diag_two, m) + part(totals, m) + transposed_product(link, across_m))
    return (
        inverse_off_one,
        inverse_diagonal_first,
        inverse_off_two,
        -jnp.concatenate(across, axis=1),
        jnp.concatenate(diag, axis=1),
    )


def local(
    root_inverse,
    lower_one,
    pattern_one,
    diag_one,
    lower_two,
    pattern_two,
    parent_two,
    lower_parent,
    diag_two,
):
    ranks_row, ranks_col = lax.axis_size("row"), lax.axis_size("col")
    row_blocks = root_inverse.shape[0] // BLOCK_SIDE
    pattern = jnp.concatenate(
        [
            pattern_one.reshape(ranks_row, row_blocks, ranks_col, -1),
            pattern_two.reshape(ranks_row, row_blocks, ranks_col, -1),
        ],
        axis=3,
    )
    pattern = pattern.transpose(0, 2, 1, 3).reshape(ranks_row, ranks_col, -1).astype(jnp.int32)
    total = pattern.shape[2]
    running = jnp.cumsum(pattern, axis=2)
    counts = running[:, :, -1:]
    rank = jnp.where(pattern > 0, running - 1, -1)
    slot = jnp.where(pattern > 0, running - 1, counts + jnp.arange(total) - running)
    order = jnp.sum(
        jnp.where(
            slot[:, :, None, :] == jnp.arange(total)[:, None],
            jnp.arange(total, dtype=jnp.int32),
            0,
        ),
        axis=3,
        dtype=jnp.int32,
    )
    levels = capacity_levels(total)
    operands = (
        (order, rank.astype(jnp.int32)),
        root_inverse,
        lower_one,
        diag_one,
        lower_two,
        parent_two,
        lower_parent,
        diag_two,
    )
    branches = [
        functools.partial(with_capacity, number, level) for number, level in enumerate(levels)
    ]
    if len(branches) == 1:
        return branches[0](*operands)
    index = jnp.sum(jnp.max(counts) > jnp.array(levels[:-1])).astype(jnp.int32)
    return lax.switch(index, branches, *operands)


def solution(mesh):
    return jax.shard_map(
        local,
        mesh=mesh,
        in_specs=(
            P(("pole", "row"), "col"),
            P(("pole", "row"), "col"),
            P(),
            P("pole", "col"),
            P(("pole", "row"), "col"),
            P(),
            P(),
            P("pole", "col"),
            P("pole", "col"),
        ),
        out_specs=(
            P(("pole", "row"), "col"),
            P("pole", "col"),
            P(("pole", "row"), "col"),
            P("pole", "col"),
            P("pole", "col"),
        ),
        check_vma=False,
    )
```

```python
import functools

import jax
import jax.numpy as jnp
from jax import lax
from jax.experimental import pallas as pl
from jax.experimental.pallas import tpu as pltpu
from jax.sharding import PartitionSpec as P

BLOCK_SIDE = 128
MODE = lax.Precision.HIGH
MESH = pl.DeviceIdType.MESH
VMEM_LIMIT = 58 * 1024 * 1024
SMEM_SPEC = pl.BlockSpec(memory_space=pltpu.SMEM)
VMEM_SPEC = pl.BlockSpec(memory_space=pltpu.VMEM)


def product(left_part, right_part):
    return jnp.dot(left_part, right_part, precision=MODE, preferred_element_type=jnp.float32)


def transposed_product(left_part, right_part):
    return lax.dot_general(
        left_part,
        right_part,
        (((0,), (0,)), ((), ())),
        precision=MODE,
        preferred_element_type=jnp.float32,
    )


def halves(value):
    high = value.astype(jnp.bfloat16)
    return high, (value - high.astype(jnp.float32)).astype(jnp.bfloat16)


def dot_f32(left, right, dims):
    left_high, left_low = halves(left)
    right_high, right_low = halves(right)
    dot = functools.partial(
        lax.dot_general,
        dimension_numbers=(dims, ((), ())),
        preferred_element_type=jnp.float32,
    )
    return dot(left_high, right_high) + (dot(left_high, right_low) + dot(left_low, right_high))


PLAIN = ((1,), (0,))
TRANSPOSED = ((0,), (0,))


def block_at(index):
    return pl.ds(pl.multiple_of(index * BLOCK_SIDE, BLOCK_SIDE), BLOCK_SIDE)


def pack_kernel(count, blocks_one, blocks_two, order_ref, one_ref, two_ref, out_ref):
    blocks = blocks_one + blocks_two

    @pl.loop(0, count)
    def _(slot):
        tile = order_ref[slot]
        rows = block_at(lax.div(tile, blocks))
        block = lax.rem(tile, blocks)

        @pl.when(block < blocks_one)
        def _():
            out_ref[slot] = one_ref[rows, block_at(block)]

        @pl.when(block >= blocks_one)
        def _():
            out_ref[slot] = two_ref[rows, block_at(block - blocks_one)]


def pack_pair(order, one, two):
    count = order.shape[0]
    return pl.pallas_call(
        functools.partial(
            pack_kernel, count, one.shape[1] // BLOCK_SIDE, two.shape[1] // BLOCK_SIDE
        ),
        out_shape=jax.ShapeDtypeStruct((count, BLOCK_SIDE, BLOCK_SIDE), jnp.float32),
        in_specs=[SMEM_SPEC, VMEM_SPEC, VMEM_SPEC],
        out_specs=VMEM_SPEC,
        compiler_params=pltpu.CompilerParams(vmem_limit_bytes=VMEM_LIMIT),
        name="pack_pair",
    )(order, one, two)


def gather_kernel(ranks_row, ranks_col, share, cuts, own_ref, plane_ref, held, *sems):
    up_send, up_recv, down_send, down_recv, side_send, side_recv, local_sem = sems
    row, col = lax.axis_index("row"), lax.axis_index("col")

    barrier = pltpu.get_barrier_semaphore()

    def greet(axes):
        pl.semaphore_signal(barrier, inc=1, device_id=axes, device_id_type=MESH)

    @pl.when(row > 0)
    def _():
        greet({"row": row - 1})

    @pl.when(row < ranks_row - 1)
    def _():
        greet({"row": row + 1})

    for step in range(1, ranks_col):
        greet({"col": lax.rem(col + step, ranks_col)})
    friends = (
        (row > 0).astype(jnp.int32) + (row < ranks_row - 1).astype(jnp.int32) + ranks_col - 1
    )
    pl.semaphore_wait(barrier, friends)

    def upward(block, piece, source):
        return pltpu.make_async_remote_copy(
            src_ref=source,
            dst_ref=held.at[block, cuts[piece]],
            send_sem=up_send.at[block, piece],
            recv_sem=up_recv.at[block, piece],
            device_id={"row": row + 1},
            device_id_type=MESH,
        )

    def downward(block, piece, source):
        return pltpu.make_async_remote_copy(
            src_ref=source,
            dst_ref=held.at[block, cuts[piece]],
            send_sem=down_send.at[block, piece],
            recv_sem=down_recv.at[block, piece],
            device_id={"row": row - 1},
            device_id_type=MESH,
        )

    def sideways(block, piece, source):
        part = lax.rem(block, share)
        return pltpu.make_async_remote_copy(
            src_ref=source,
            dst_ref=plane_ref.at[col, part, cuts[piece]],
            send_sem=side_send.at[block, piece],
            recv_sem=side_recv.at[col, part, piece],
            device_id={"col": lax.div(block, share)},
            device_id_type=MESH,
        )

    def inward(block, piece, source):
        part = lax.rem(block, share)
        return pltpu.make_async_copy(
            source, plane_ref.at[col, part, cuts[piece]], local_sem.at[part, piece]
        )

    def deliver(block, piece, source):
        @pl.when(lax.div(block, share) != col)
        def _():
            sideways(block, piece, source).start()

        @pl.when(lax.div(block, share) == col)
        def _():
            inward(block, piece, source).start()

    pieces = range(len(cuts))
    for piece in pieces:
        source = own_ref.at[cuts[piece]]

        @pl.when(row < ranks_row - 1)
        def _():
            upward(row, piece, source).start()

        @pl.when(row > 0)
        def _():
            downward(row, piece, source).start()

        deliver(row, piece, source)

    @pl.loop(1, ranks_row)
    def _(step):
        for piece in pieces:
            below, above = row - step, row + step

            @pl.when(below >= 0)
            def _():
                source = held.at[below, cuts[piece]]
                upward(below, piece, source).wait_recv()

                @pl.when(row < ranks_row - 1)
                def _():
                    upward(below, piece, source).start()

                deliver(below, piece, source)

            @pl.when(above < ranks_row)
            def _():
                source = held.at[above, cuts[piece]]
                downward(above, piece, source).wait_recv()

                @pl.when(row > 0)
                def _():
                    downward(above, piece, source).start()

                deliver(above, piece, source)

    @pl.loop(0, ranks_row)
    def _(block):
        for piece in pieces:
            source = own_ref.at[cuts[piece]]

            @pl.when(jnp.logical_and(block <= row, row < ranks_row - 1))
            def _():
                upward(block, piece, source).wait_send()

            @pl.when(jnp.logical_and(block >= row, row > 0))
            def _():
                downward(block, piece, source).wait_send()

            @pl.when(lax.div(block, share) != col)
            def _():
                sideways(block, piece, source).wait_send()

            @pl.when(lax.div(block, share) == col)
            def _():
                inward(block, piece, source).wait()

    @pl.loop(0, share)
    def _(part):
        for piece in pieces:
            source = own_ref.at[cuts[piece]]
            for step in range(1, ranks_col):
                other = lax.rem(col + step, ranks_col)
                pltpu.make_async_remote_copy(
                    src_ref=source,
                    dst_ref=plane_ref.at[other, part, cuts[piece]],
                    send_sem=side_send.at[0, piece],
                    recv_sem=side_recv.at[other, part, piece],
                    device_id={"col": other},
                    device_id_type=MESH,
                ).wait_recv()


def gather_plane(packed, collective):
    ranks_row, ranks_col = lax.axis_size("row"), lax.axis_size("col")
    share = ranks_row // ranks_col
    count = packed.shape[0]
    pieces = min(4, count)
    edges = [count * piece // pieces for piece in range(pieces + 1)]
    cuts = [pl.ds(low, high - low) for low, high in zip(edges[:-1], edges[1:])]
    by_row = pltpu.SemaphoreType.DMA((ranks_row, pieces))
    return pl.pallas_call(
        functools.partial(gather_kernel, ranks_row, ranks_col, share, cuts),
        out_shape=jax.ShapeDtypeStruct((ranks_col, share) + packed.shape, packed.dtype),
        in_specs=[VMEM_SPEC],
        out_specs=VMEM_SPEC,
        scratch_shapes=[
            pltpu.VMEM((ranks_row,) + packed.shape, packed.dtype),
            by_row,
            by_row,
            by_row,
            by_row,
            by_row,
            pltpu.SemaphoreType.DMA((ranks_col, share, pieces)),
            pltpu.SemaphoreType.DMA((share, pieces)),
        ],
        compiler_params=pltpu.CompilerParams(
            collective_id=collective, has_side_effects=True, vmem_limit_bytes=VMEM_LIMIT
        ),
        name="gather_plane",
    )(packed)


def fours_and_twos(count):
    left = lax.rem(count, 4)
    return (
        lax.div(count, 4) + (left > 2).astype(jnp.int32),
        jnp.logical_and(left > 0, left <= 2).astype(jnp.int32),
    )


def multiply_kernel(
    row_blocks,
    col_blocks,
    columns,
    tiles,
    place_ref,
    slot_ref,
    left_ref,
    plane_ref,
    out_ref,
    split,
    inner_list,
    inner_place,
    outer_list,
):
    split[tiles] = jnp.zeros_like(split[tiles])

    @pl.loop(0, tiles)
    def _(tile):
        high, low = halves(plane_ref[tile])
        split[tile] = jnp.concatenate([high, low], axis=1)

    @pl.loop(0, columns)
    def _(column):
        def scan_inner(block, found):
            place = place_ref[block * columns + column]

            @pl.when(place >= 0)
            def _():
                inner_list[found] = block
                inner_place[found] = place

            return found + (place >= 0).astype(jnp.int32)

        inner = lax.fori_loop(0, col_blocks, scan_inner, jnp.int32(0))
        for n in range(3):
            inner_list[inner + n] = 0
            inner_place[inner + n] = tiles

        def scan_outer(block, found):
            kept = slot_ref[block * columns + column] >= 0

            @pl.when(kept)
            def _():
                outer_list[found] = block

            return found + kept.astype(jnp.int32)

        outer = lax.fori_loop(0, row_blocks, scan_outer, jnp.int32(0))

        def outer_group(start, height):
            rows = [outer_list[jnp.minimum(start + n, outer - 1)] for n in range(height)]

            def step(start_inner, depth, total):
                cols = [inner_list[start_inner + n] for n in range(depth)]
                left = jnp.concatenate(
                    [
                        jnp.concatenate(
                            [left_ref[block_at(i), block_at(j)] for j in cols], axis=1
                        )
                        for i in rows
                    ],
                    axis=0,
                )
                high, low = halves(left)
                right = jnp.concatenate(
                    [split[inner_place[start_inner + n]] for n in range(depth)], axis=0
                )
                wide = jnp.dot(high, right, preferred_element_type=jnp.float32)
                narrow = jnp.dot(low, right[:, :BLOCK_SIDE], preferred_element_type=jnp.float32)
                return total + (wide[:, :BLOCK_SIDE] + (wide[:, BLOCK_SIDE:] + narrow))

            total = jnp.zeros((height * BLOCK_SIDE, BLOCK_SIDE), jnp.float32)
            total = lax.fori_loop(0, inner_fours, lambda n, t: step(4 * n, 4, t), total)
            total = lax.fori_loop(0, inner_twos, lambda n, t: step(4 * inner_fours, 2, t), total)
            for n, i in enumerate(rows):
                out_ref[slot_ref[i * columns + column]] = total[
                    n * BLOCK_SIDE : (n + 1) * BLOCK_SIDE
                ]

        inner_fours, inner_twos = fours_and_twos(inner)
        outer_fours, outer_twos = fours_and_twos(outer)

        @pl.loop(0, outer_fours)
        def _(group):
            outer_group(4 * group, 4)

        @pl.loop(0, outer_twos)
        def _(group):
            outer_group(4 * outer_fours, 2)


def multiply_tiles(place, slot, left, plane, count):
    col_blocks, columns = place.shape
    row_blocks = slot.shape[0]
    tiles = plane.shape[0]
    return pl.pallas_call(
        functools.partial(multiply_kernel, row_blocks, col_blocks, columns, tiles),
        out_shape=jax.ShapeDtypeStruct((count, BLOCK_SIDE, BLOCK_SIDE), jnp.float32),
        in_specs=[SMEM_SPEC, SMEM_SPEC, VMEM_SPEC, VMEM_SPEC],
        out_specs=VMEM_SPEC,
        scratch_shapes=[
            pltpu.VMEM((tiles + 1, BLOCK_SIDE, 2 * BLOCK_SIDE), jnp.bfloat16),
            pltpu.SMEM((col_blocks + 4,), jnp.int32),
            pltpu.SMEM((col_blocks + 4,), jnp.int32),
            pltpu.SMEM((row_blocks + 2,), jnp.int32),
        ],
        compiler_params=pltpu.CompilerParams(vmem_limit_bytes=VMEM_LIMIT),
        name="multiply_tiles",
    )(place.reshape(-1), slot.reshape(-1), left, plane)


def finish_kernel(
    ranks_row,
    ranks_col,
    cuts,
    capacity_one,
    sizes,
    rank_ref,
    parent_place_ref,
    parent_block_ref,
    parts_ref,
    one_ref,
    two_ref,
    link_ref,
    diag_one_ref,
    diag_two_ref,
    off_one_ref,
    off_two_ref,
    final_ref,
    near,
    both,
    far,
    level_one,
    summed,
    inner_own,
    all_one,
    all_inner,
    dense,
    solved,
    parent,
    sums,
    reduced,
    *sems,
):
    near_send, near_recv, far_send, far_recv = sems[:4]
    one_send, one_recv, inner_send, inner_recv = sems[4:8]
    fold_send, fold_recv, last_send, last_recv = sems[8:]
    row_blocks, blocks_one, blocks_two = sizes
    blocks = blocks_one + blocks_two
    groups = ranks_col // 2
    owners = last_recv.shape[0]
    row, col = lax.axis_index("row"), lax.axis_index("col")
    group, parity = lax.div(col, 2), lax.rem(col, 2)
    sibling = 2 * group + 1 - parity
    others = [lax.rem(group + step, groups) for step in range(1, groups)]
    pieces = range(len(cuts))

    barrier = pltpu.get_barrier_semaphore()
    pl.semaphore_signal(barrier, inc=1, device_id={"col": sibling}, device_id_type=MESH)
    for other in others:
        pl.semaphore_signal(
            barrier, inc=1, device_id={"col": 2 * other + parity}, device_id_type=MESH
        )

    @pl.loop(1, ranks_row)
    def _(step):
        pl.semaphore_signal(
            barrier,
            inc=1,
            device_id={"row": lax.rem(row + step, ranks_row)},
            device_id_type=MESH,
        )

    pl.semaphore_wait(barrier, groups + ranks_row - 1)

    def remote(source, target, send, recv, device):
        return pltpu.make_async_remote_copy(
            src_ref=source,
            dst_ref=target,
            send_sem=send,
            recv_sem=recv,
            device_id=device,
            device_id_type=MESH,
        )

    def to_sibling(to_group, piece):
        return remote(
            parts_ref.at[2 * to_group + 1 - parity, cuts[piece]],
            near.at[to_group, cuts[piece]],
            near_send.at[to_group, piece],
            near_recv.at[to_group, piece],
            {"col": sibling},
        )

    def to_group(other, piece):
        return remote(
            both.at[other, cuts[piece]],
            far.at[group, cuts[piece]],
            far_send.at[other, piece],
            far_recv.at[group, piece],
            {"col": 2 * other + parity},
        )

    def from_group(other, piece):
        return remote(
            both.at[other, cuts[piece]],
            far.at[other, cuts[piece]],
            far_send.at[other, piece],
            far_recv.at[other, piece],
            {"col": 2 * other + parity},
        )

    for piece in pieces:
        for other in others + [group]:
            to_sibling(other, piece).start()
    for piece in pieces:
        for other in others:
            to_sibling(other, piece).wait_recv()

            @pl.loop(cuts[piece].start, cuts[piece].start + cuts[piece].size)
            def _(tile):
                both[other, tile] = parts_ref[2 * other + parity, tile] + near[other, tile]

            to_group(other, piece).start()

    def total_of(piece, target):
        to_sibling(group, piece).wait_recv()
        for other in others:
            from_group(other, piece).wait_recv()

        @pl.loop(cuts[piece].start, cuts[piece].start + cuts[piece].size)
        def _(tile):
            total = parts_ref[col, tile] + near[group, tile]
            for other in others:
                total = total + far[other, tile]
            target[tile] = total

    def spread_one(source, target, send, recv):
        copies = [remote(source, target.at[col], send.at[0], recv.at[col], {"col": sibling})]
        for number, other in enumerate(others):
            copies.append(
                remote(
                    source,
                    target.at[col],
                    send.at[1 + number],
                    recv.at[col],
                    {"col": 2 * other + parity},
                )
            )
        return copies

    total_of(0, level_one)
    one_copies = spread_one(level_one, all_one, one_send, one_recv)
    for copy in one_copies:
        copy.start()

    chunk = min(row_blocks, 4)
    for k in range(blocks_one):
        cols = pl.ds(k * BLOCK_SIDE, BLOCK_SIDE)

        @pl.loop(0, row_blocks)
        def _(block):
            rank = rank_ref[block * blocks + k]
            tile = jnp.where(rank >= 0, level_one[jnp.maximum(rank, 0)], 0.0)
            dense[block_at(block)] = tile
            off_one_ref[block_at(block), cols] = -tile

        first_row = (row == 0).astype(jnp.float32)
        inner_own[k] = first_row * diag_one_ref[:, cols]

        @pl.loop(0, row_blocks // chunk)
        def _(part):
            rows = pl.ds(
                pl.multiple_of(part * (chunk * BLOCK_SIDE), BLOCK_SIDE), chunk * BLOCK_SIDE
            )
            inner_own[k] += dot_f32(one_ref[rows, cols], dense[rows], TRANSPOSED)

    inner_copies = spread_one(inner_own, all_inner, inner_send, inner_recv)
    for copy in inner_copies:
        copy.start()

    for piece in pieces[1:]:
        total_of(piece, summed)

    forwards = []
    for source, target, send, recv in (
        (level_one, all_one, one_send, one_recv),
        (inner_own, all_inner, inner_send, inner_recv),
    ):
        for number, other in enumerate(others):
            origin = 2 * other + parity
            remote(source, target.at[origin], send.at[0], recv.at[origin], {"col": sibling}).wait_recv()
            forward = remote(
                target.at[origin],
                target.at[origin],
                send.at[groups + number],
                recv.at[origin],
                {"col": sibling},
            )
            forward.start()
            forwards.append(forward)
    for source, target, send, recv in (
        (level_one, all_one, one_send, one_recv),
        (inner_own, all_inner, inner_send, inner_recv),
    ):
        for other in others + [group]:
            origin = 2 * other + 1 - parity
            remote(source, target.at[origin], send.at[0], recv.at[origin], {"col": sibling}).wait_recv()

    @pl.loop(0, capacity_one)
    def _(tile):
        all_one[col, tile] = level_one[tile]
        summed[tile] = level_one[tile]

    for k in range(blocks_one):
        all_inner[col, k] = inner_own[k]

    for m in range(blocks_two):
        cols = pl.ds(m * BLOCK_SIDE, BLOCK_SIDE)
        link = link_ref[:, cols]
        across_cols = cols
        diag_cols = pl.ds((blocks_two + m) * BLOCK_SIDE, BLOCK_SIDE)
        sums[:, across_cols] = jnp.zeros((BLOCK_SIDE, BLOCK_SIDE), jnp.float32)
        sums[:, diag_cols] = (row == 0).astype(jnp.float32) * diag_two_ref[:, cols]

        @pl.loop(0, row_blocks)
        def _(block):
            rank = rank_ref[block * blocks + blocks_one + m]
            place = parent_place_ref[block * blocks_two + m]
            keep = rank >= 0
            rows = block_at(block)
            tile = all_one[lax.div(place, capacity_one), lax.rem(place, capacity_one)]
            parent[rows] = jnp.where(keep, tile, 0.0)
            solved[rows] = jnp.where(keep, summed[jnp.maximum(rank, 0)], 0.0)
            dense[rows] = jnp.where(keep, two_ref[rows, cols], 0.0)

        @pl.loop(0, row_blocks // chunk)
        def _(part):
            rows = pl.ds(
                pl.multiple_of(part * (chunk * BLOCK_SIDE), BLOCK_SIDE), chunk * BLOCK_SIDE
            )
            above = parent[rows]
            here = solved[rows] - dot_f32(above, link, PLAIN)
            off_two_ref[rows, cols] = -here
            factor = dense[rows]
            sums[:, diag_cols] += dot_f32(factor, here, TRANSPOSED)
            sums[:, across_cols] -= dot_f32(above, factor, TRANSPOSED)

        block = parent_block_ref[m]
        across = sums[:, across_cols] + dot_f32(
            all_inner[lax.div(block, blocks_one), lax.rem(block, blocks_one)], link, PLAIN
        )
        sums[:, across_cols] = across
        sums[:, diag_cols] += dot_f32(link, across, TRANSPOSED)
    for k in range(blocks_one):
        sums[:, pl.ds((2 * blocks_two + k) * BLOCK_SIDE, BLOCK_SIDE)] = inner_own[k]

    height = BLOCK_SIDE // owners

    def band(owner):
        return pl.ds(pl.multiple_of(owner * height, height), height)

    def fold(owner, origin):
        return remote(
            sums.at[band(owner)],
            reduced.at[origin],
            fold_send.at[owner],
            fold_recv.at[origin],
            {"row": owner},
        )

    @pl.loop(0, owners)
    def _(owner):
        @pl.when(owner != row)
        def _():
            fold(owner, row).start()

    @pl.when(row < owners)
    def _():
        @pl.loop(1, ranks_row)
        def _(step):
            origin = lax.rem(row + step, ranks_row)
            remote(
                sums.at[band(row)],
                reduced.at[origin],
                fold_send.at[0],
                fold_recv.at[origin],
                {"row": origin},
            ).wait_recv()

        reduced[row] = sums[band(row)]
        final_ref[band(row)] = reduced[0]

        @pl.loop(1, ranks_row)
        def _(origin):
            final_ref[band(row)] += reduced[origin]

        @pl.loop(1, ranks_row)
        def _(step):
            target = lax.rem(row + step, ranks_row)
            remote(
                final_ref.at[band(row)],
                final_ref.at[band(row)],
                last_send.at[target],
                last_recv.at[row],
                {"row": target},
            ).start()

    @pl.loop(0, owners)
    def _(owner):
        @pl.when(owner != row)
        def _():
            fold(owner, row).wait_send()
            remote(
                final_ref.at[band(owner)],
                final_ref.at[band(owner)],
                last_send.at[0],
                last_recv.at[owner],
                {"row": owner},
            ).wait_recv()

    @pl.when(row < owners)
    def _():
        @pl.loop(1, ranks_row)
        def _(step):
            target = lax.rem(row + step, ranks_row)
            remote(
                final_ref.at[band(row)],
                final_ref.at[band(row)],
                last_send.at[target],
                last_recv.at[row],
                {"row": target},
            ).wait_send()

    for piece in pieces:
        for other in others + [group]:
            to_sibling(other, piece).wait_send()
        for other in others:
            to_group(other, piece).wait_send()
    for copy in one_copies + inner_copies + forwards:
        copy.wait_send()


def finish(
    rank, parent_place, parent_block, parts, one, two, link, diag_one, diag_two, levels, collective
):
    ranks_row, ranks_col = lax.axis_size("row"), lax.axis_size("col")
    capacity, capacity_one = levels
    row_blocks, blocks = rank.shape
    blocks_one, blocks_two = one.shape[1] // BLOCK_SIDE, two.shape[1] // BLOCK_SIDE
    groups = ranks_col // 2
    owners = min(ranks_row, BLOCK_SIDE // 8)
    middle = (capacity_one + capacity + 1) // 2
    edges = [0, capacity_one, middle, capacity]
    if middle >= capacity:
        edges = [0, capacity_one, capacity]
    cuts = [pl.ds(low, high - low) for low, high in zip(edges[:-1], edges[1:])]
    width = (2 * blocks_two + blocks_one) * BLOCK_SIDE
    tile = (BLOCK_SIDE, BLOCK_SIDE)
    by_piece = pltpu.SemaphoreType.DMA((groups, len(cuts)))
    by_copy = pltpu.SemaphoreType.DMA((2 * groups,))
    by_col = pltpu.SemaphoreType.DMA((ranks_col,))
    by_row = pltpu.SemaphoreType.DMA((ranks_row,))
    by_owner = pltpu.SemaphoreType.DMA((owners,))
    return pl.pallas_call(
        functools.partial(
            finish_kernel,
            ranks_row,
            ranks_col,
            cuts,
            capacity_one,
            (row_blocks, blocks_one, blocks_two),
        ),
        out_shape=(
            jax.ShapeDtypeStruct(one.shape, jnp.float32),
            jax.ShapeDtypeStruct(two.shape, jnp.float32),
            jax.ShapeDtypeStruct((BLOCK_SIDE, width), jnp.float32),
        ),
        in_specs=[SMEM_SPEC] * 3 + [VMEM_SPEC] * 6,
        out_specs=(VMEM_SPEC,) * 3,
        scratch_shapes=[
            pltpu.VMEM((groups, capacity) + tile, jnp.float32),
            pltpu.VMEM((groups, capacity) + tile, jnp.float32),
            pltpu.VMEM((groups, capacity) + tile, jnp.float32),
            pltpu.VMEM((capacity_one,) + tile, jnp.float32),
            pltpu.VMEM((capacity,) + tile, jnp.float32),
            pltpu.VMEM((blocks_one,) + tile, jnp.float32),
            pltpu.VMEM((ranks_col, capacity_one) + tile, jnp.float32),
            pltpu.VMEM((ranks_col, blocks_one) + tile, jnp.float32),
            pltpu.VMEM((row_blocks * BLOCK_SIDE, BLOCK_SIDE), jnp.float32),
            pltpu.VMEM((row_blocks * BLOCK_SIDE, BLOCK_SIDE), jnp.float32),
            pltpu.VMEM((row_blocks * BLOCK_SIDE, BLOCK_SIDE), jnp.float32),
            pltpu.VMEM((BLOCK_SIDE, width), jnp.float32),
            pltpu.VMEM((ranks_row, BLOCK_SIDE // owners, width), jnp.float32),
            by_piece,
            by_piece,
            by_piece,
            by_piece,
            by_copy,
            by_col,
            by_copy,
            by_col,
            by_owner,
            by_row,
            by_row,
            by_owner,
        ],
        compiler_params=pltpu.CompilerParams(
            collective_id=collective, has_side_effects=True, vmem_limit_bytes=VMEM_LIMIT
        ),
        name="finish",
    )(
        rank.reshape(-1),
        parent_place.reshape(-1),
        parent_block,
        parts.reshape((ranks_col, capacity) + tile),
        one,
        two,
        link,
        diag_one,
        diag_two,
    )


def capacity_levels(total, total_one):
    full = (total, total_one)
    if total < 16:
        return (full,)
    parts = ((11, 16), (12, 17), (13, 18), (14, 20))
    return tuple((-(-total * p // 24), -(-total_one * q // 24)) for p, q in parts) + (full,)


def with_capacity(
    collective,
    levels,
    tables,
    root_inverse,
    lower_one,
    diag_one,
    lower_two,
    parent_two,
    lower_parent,
    diag_two,
):
    order, rank = tables
    capacity, capacity_one = levels
    ranks_row, ranks_col, total = order.shape
    row, col = lax.axis_index("row"), lax.axis_index("col")
    rows_here, cols_here = root_inverse.shape
    row_blocks = rows_here // BLOCK_SIDE
    col_one, col_two = (
        lower_one.shape[1] // BLOCK_SIDE,
        lower_two.shape[1] // BLOCK_SIDE,
    )
    blocks = col_one + col_two
    share = ranks_row // ranks_col

    own = lax.dynamic_index_in_dim(
        lax.dynamic_index_in_dim(order, row, 0, False), col, 0, False
    )[:capacity]
    plane = gather_plane(pack_pair(own, lower_one, lower_two), 2 * collective)

    here = lax.dynamic_slice_in_dim(rank, col * share, share, 0)
    base = (
        jnp.arange(ranks_col, dtype=jnp.int32)[None, :, None] * share
        + jnp.arange(share, dtype=jnp.int32)[:, None, None]
    ) * capacity
    place = jnp.where(here >= 0, here + base, -1).reshape(share, ranks_col, row_blocks, blocks)
    place = place.transpose(0, 2, 1, 3).reshape(share * row_blocks, ranks_col * blocks)
    mine = lax.dynamic_index_in_dim(rank, row, 0, False)
    start = jnp.arange(ranks_col, dtype=jnp.int32)[:, None] * capacity
    slot = jnp.where(mine >= 0, mine + start, -1).reshape(ranks_col, row_blocks, blocks)
    slot = slot.transpose(1, 0, 2).reshape(row_blocks, ranks_col * blocks)
    partial_sum = multiply_tiles(
        place,
        slot,
        root_inverse,
        plane.reshape(-1, BLOCK_SIDE, BLOCK_SIDE),
        ranks_col * capacity,
    )
    own_rank = lax.dynamic_index_in_dim(mine, col, 0, False).reshape(row_blocks, blocks)
    parents = lax.dynamic_slice_in_dim(parent_two, col * col_two, col_two, 0)
    first = mine.reshape(ranks_col, row_blocks, blocks)[:, :, :col_one]
    first = first + jnp.arange(ranks_col, dtype=jnp.int32)[:, None, None] * capacity_one
    first = first.transpose(1, 0, 2).reshape(row_blocks, ranks_col * col_one)
    parent_place = jnp.where(own_rank[:, col_one:] >= 0, jnp.take(first, parents, axis=1), 0)
    inverse_off_one, inverse_off_two, final = finish(
        own_rank,
        parent_place,
        parents,
        partial_sum,
        lower_one,
        lower_two,
        lower_parent,
        diag_one,
        diag_two,
        levels,
        2 * collective + 1,
    )
    width = col_two * BLOCK_SIDE
    return (
        inverse_off_one,
        final[:, 2 * width :],
        inverse_off_two,
        -final[:, :width],
        final[:, width : 2 * width],
    )


def local(
    root_inverse,
    lower_one,
    pattern_one,
    diag_one,
    lower_two,
    pattern_two,
    parent_two,
    lower_parent,
    diag_two,
):
    ranks_row, ranks_col = lax.axis_size("row"), lax.axis_size("col")
    row_blocks = root_inverse.shape[0] // BLOCK_SIDE
    pattern = jnp.concatenate(
        [
            pattern_one.reshape(ranks_row, row_blocks, ranks_col, -1),
            pattern_two.reshape(ranks_row, row_blocks, ranks_col, -1),
        ],
        axis=3,
    )
    pattern = pattern.transpose(0, 2, 1, 3).reshape(ranks_row, ranks_col, -1).astype(jnp.int32)
    total = pattern.shape[2]
    blocks_one = pattern_one.shape[1] // ranks_col
    grid = pattern.reshape(ranks_row, ranks_col, row_blocks, -1)
    one = grid[..., :blocks_one].reshape(ranks_row, ranks_col, -1)
    two = grid[..., blocks_one:].reshape(ranks_row, ranks_col, -1)
    counts_one = jnp.sum(one, axis=2, keepdims=True)
    running = jnp.concatenate(
        [
            jnp.cumsum(one, axis=2).reshape(ranks_row, ranks_col, row_blocks, -1),
            (counts_one + jnp.cumsum(two, axis=2)).reshape(ranks_row, ranks_col, row_blocks, -1),
        ],
        axis=3,
    ).reshape(ranks_row, ranks_col, total)
    counts = counts_one + jnp.sum(two, axis=2, keepdims=True)
    rank = jnp.where(pattern > 0, running - 1, -1)
    order = jnp.sum(
        jnp.where(
            rank[:, :, None, :] == jnp.arange(total)[:, None],
            jnp.arange(total, dtype=jnp.int32),
            0,
        ),
        axis=3,
        dtype=jnp.int32,
    )
    levels = capacity_levels(total, row_blocks * blocks_one)
    operands = (
        (order, rank.astype(jnp.int32)),
        root_inverse,
        lower_one,
        diag_one,
        lower_two,
        parent_two,
        lower_parent,
        diag_two,
    )
    branches = [
        functools.partial(with_capacity, number, level) for number, level in enumerate(levels)
    ]
    if len(branches) == 1:
        return branches[0](*operands)
    peak = jnp.stack([jnp.max(counts), jnp.max(counts_one)])
    over = jnp.any(peak > jnp.array(levels[:-1], dtype=jnp.int32), axis=1)
    index = jnp.sum(over).astype(jnp.int32)
    return lax.switch(index, branches, *operands)


def solution(mesh):
    return jax.shard_map(
        local,
        mesh=mesh,
        in_specs=(
            P(("pole", "row"), "col"),
            P(("pole", "row"), "col"),
            P(),
            P("pole", "col"),
            P(("pole", "row"), "col"),
            P(),
            P(),
            P("pole", "col"),
            P("pole", "col"),
        ),
        out_specs=(
            P(("pole", "row"), "col"),
            P("pole", "col"),
            P(("pole", "row"), "col"),
            P("pole", "col"),
            P("pole", "col"),
        ),
        check_vma=False,
    )
```

```python
import functools

import jax
import jax.numpy as jnp
import numpy as np
from jax import lax
from jax.experimental import pallas as pl
from jax.experimental.pallas import tpu as pltpu
from jax.sharding import PartitionSpec as P

BLOCK_SIDE = 128
MODE = lax.Precision.HIGH
MESH = pl.DeviceIdType.MESH
VMEM_LIMIT = 58 * 1024 * 1024
SMEM_SPEC = pl.BlockSpec(memory_space=pltpu.SMEM)
VMEM_SPEC = pl.BlockSpec(memory_space=pltpu.VMEM)


def product(left_part, right_part):
    return jnp.dot(left_part, right_part, precision=MODE, preferred_element_type=jnp.float32)


def transposed_product(left_part, right_part):
    return lax.dot_general(
        left_part,
        right_part,
        (((0,), (0,)), ((), ())),
        precision=MODE,
        preferred_element_type=jnp.float32,
    )


def halves(value):
    high = value.astype(jnp.bfloat16)
    return high, (value - high.astype(jnp.float32)).astype(jnp.bfloat16)


def dot_f32(left, right, dims):
    left_high, left_low = halves(left)
    right_high, right_low = halves(right)
    dot = functools.partial(
        lax.dot_general,
        dimension_numbers=(dims, ((), ())),
        preferred_element_type=jnp.float32,
    )
    return dot(left_high, right_high) + (dot(left_high, right_low) + dot(left_low, right_high))


PLAIN = ((1,), (0,))
TRANSPOSED = ((0,), (0,))


def block_at(index):
    return pl.ds(pl.multiple_of(index * BLOCK_SIDE, BLOCK_SIDE), BLOCK_SIDE)


def pack_kernel(count, blocks_one, blocks_two, order_ref, one_ref, two_ref, out_ref):
    blocks = blocks_one + blocks_two

    @pl.loop(0, count)
    def _(slot):
        tile = order_ref[slot]
        rows = block_at(lax.div(tile, blocks))
        block = lax.rem(tile, blocks)

        @pl.when(block < blocks_one)
        def _():
            out_ref[slot] = one_ref[rows, block_at(block)]

        @pl.when(block >= blocks_one)
        def _():
            out_ref[slot] = two_ref[rows, block_at(block - blocks_one)]


def pack_pair(order, one, two):
    count = order.shape[0]
    return pl.pallas_call(
        functools.partial(
            pack_kernel, count, one.shape[1] // BLOCK_SIDE, two.shape[1] // BLOCK_SIDE
        ),
        out_shape=jax.ShapeDtypeStruct((count, BLOCK_SIDE, BLOCK_SIDE), jnp.float32),
        in_specs=[SMEM_SPEC, VMEM_SPEC, VMEM_SPEC],
        out_specs=VMEM_SPEC,
        compiler_params=pltpu.CompilerParams(vmem_limit_bytes=VMEM_LIMIT),
        name="pack_pair",
    )(order, one, two)


def gather_kernel(ranks_row, ranks_col, share, cuts, own_ref, plane_ref, held, *sems):
    up_send, up_recv, down_send, down_recv, side_send, side_recv, local_sem = sems
    row, col = lax.axis_index("row"), lax.axis_index("col")

    barrier = pltpu.get_barrier_semaphore()

    def greet(axes):
        pl.semaphore_signal(barrier, inc=1, device_id=axes, device_id_type=MESH)

    @pl.when(row > 0)
    def _():
        greet({"row": row - 1})

    @pl.when(row < ranks_row - 1)
    def _():
        greet({"row": row + 1})

    for step in range(1, ranks_col):
        greet({"col": lax.rem(col + step, ranks_col)})
    friends = (
        (row > 0).astype(jnp.int32) + (row < ranks_row - 1).astype(jnp.int32) + ranks_col - 1
    )
    pl.semaphore_wait(barrier, friends)

    def upward(block, piece, source):
        return pltpu.make_async_remote_copy(
            src_ref=source,
            dst_ref=held.at[block, cuts[piece]],
            send_sem=up_send.at[block, piece],
            recv_sem=up_recv.at[block, piece],
            device_id={"row": row + 1},
            device_id_type=MESH,
        )

    def downward(block, piece, source):
        return pltpu.make_async_remote_copy(
            src_ref=source,
            dst_ref=held.at[block, cuts[piece]],
            send_sem=down_send.at[block, piece],
            recv_sem=down_recv.at[block, piece],
            device_id={"row": row - 1},
            device_id_type=MESH,
        )

    def sideways(block, piece, source):
        part = lax.rem(block, share)
        return pltpu.make_async_remote_copy(
            src_ref=source,
            dst_ref=plane_ref.at[col, part, cuts[piece]],
            send_sem=side_send.at[block, piece],
            recv_sem=side_recv.at[col, part, piece],
            device_id={"col": lax.div(block, share)},
            device_id_type=MESH,
        )

    def inward(block, piece, source):
        part = lax.rem(block, share)
        return pltpu.make_async_copy(
            source, plane_ref.at[col, part, cuts[piece]], local_sem.at[part, piece]
        )

    def deliver(block, piece, source):
        @pl.when(lax.div(block, share) != col)
        def _():
            sideways(block, piece, source).start()

        @pl.when(lax.div(block, share) == col)
        def _():
            inward(block, piece, source).start()

    pieces = range(len(cuts))
    for piece in pieces:
        source = own_ref.at[cuts[piece]]

        @pl.when(row < ranks_row - 1)
        def _():
            upward(row, piece, source).start()

        @pl.when(row > 0)
        def _():
            downward(row, piece, source).start()

        deliver(row, piece, source)

    @pl.loop(1, ranks_row)
    def _(step):
        for piece in pieces:
            below, above = row - step, row + step

            @pl.when(below >= 0)
            def _():
                source = held.at[below, cuts[piece]]
                upward(below, piece, source).wait_recv()

                @pl.when(row < ranks_row - 1)
                def _():
                    upward(below, piece, source).start()

                deliver(below, piece, source)

            @pl.when(above < ranks_row)
            def _():
                source = held.at[above, cuts[piece]]
                downward(above, piece, source).wait_recv()

                @pl.when(row > 0)
                def _():
                    downward(above, piece, source).start()

                deliver(above, piece, source)

    @pl.loop(0, ranks_row)
    def _(block):
        for piece in pieces:
            source = own_ref.at[cuts[piece]]

            @pl.when(jnp.logical_and(block <= row, row < ranks_row - 1))
            def _():
                upward(block, piece, source).wait_send()

            @pl.when(jnp.logical_and(block >= row, row > 0))
            def _():
                downward(block, piece, source).wait_send()

            @pl.when(lax.div(block, share) != col)
            def _():
                sideways(block, piece, source).wait_send()

            @pl.when(lax.div(block, share) == col)
            def _():
                inward(block, piece, source).wait()

    @pl.loop(0, share)
    def _(part):
        for piece in pieces:
            source = own_ref.at[cuts[piece]]
            for step in range(1, ranks_col):
                other = lax.rem(col + step, ranks_col)
                pltpu.make_async_remote_copy(
                    src_ref=source,
                    dst_ref=plane_ref.at[other, part, cuts[piece]],
                    send_sem=side_send.at[0, piece],
                    recv_sem=side_recv.at[other, part, piece],
                    device_id={"col": other},
                    device_id_type=MESH,
                ).wait_recv()


def gather_plane(packed, collective):
    ranks_row, ranks_col = lax.axis_size("row"), lax.axis_size("col")
    share = ranks_row // ranks_col
    count = packed.shape[0]
    pieces = min(6, count)
    edges = [count * piece // pieces for piece in range(pieces + 1)]
    cuts = [pl.ds(low, high - low) for low, high in zip(edges[:-1], edges[1:])]
    by_row = pltpu.SemaphoreType.DMA((ranks_row, pieces))
    return pl.pallas_call(
        functools.partial(gather_kernel, ranks_row, ranks_col, share, cuts),
        out_shape=jax.ShapeDtypeStruct((ranks_col, share) + packed.shape, packed.dtype),
        in_specs=[VMEM_SPEC],
        out_specs=VMEM_SPEC,
        scratch_shapes=[
            pltpu.VMEM((ranks_row,) + packed.shape, packed.dtype),
            by_row,
            by_row,
            by_row,
            by_row,
            by_row,
            pltpu.SemaphoreType.DMA((ranks_col, share, pieces)),
            pltpu.SemaphoreType.DMA((share, pieces)),
        ],
        compiler_params=pltpu.CompilerParams(
            collective_id=collective, has_side_effects=True, vmem_limit_bytes=VMEM_LIMIT
        ),
        name="gather_plane",
    )(packed)


def fours_and_twos(count):
    left = lax.rem(count, 4)
    return (
        lax.div(count, 4) + (left > 2).astype(jnp.int32),
        jnp.logical_and(left > 0, left <= 2).astype(jnp.int32),
    )


def multiply_kernel(
    row_blocks,
    col_blocks,
    columns,
    tiles,
    place_ref,
    slot_ref,
    left_hbm,
    plane_ref,
    out_ref,
    left_ref,
    left_sem,
    split,
    inner_list,
    inner_place,
    outer_list,
):
    left_copy = pltpu.make_async_copy(left_hbm, left_ref, left_sem)
    left_copy.start()
    split[tiles] = jnp.zeros_like(split[tiles])

    @pl.loop(0, tiles)
    def _(tile):
        high, low = halves(plane_ref[tile])
        split[tile] = jnp.concatenate([high, low], axis=1)

    left_copy.wait()

    @pl.loop(0, columns)
    def _(column):
        def scan_inner(block, found):
            place = place_ref[block * columns + column]

            @pl.when(place >= 0)
            def _():
                inner_list[found] = block
                inner_place[found] = place

            return found + (place >= 0).astype(jnp.int32)

        inner = lax.fori_loop(0, col_blocks, scan_inner, jnp.int32(0))
        for n in range(3):
            inner_list[inner + n] = 0
            inner_place[inner + n] = tiles

        def scan_outer(block, found):
            kept = slot_ref[block * columns + column] >= 0

            @pl.when(kept)
            def _():
                outer_list[found] = block

            return found + kept.astype(jnp.int32)

        outer = lax.fori_loop(0, row_blocks, scan_outer, jnp.int32(0))

        def outer_group(start, height):
            rows = [outer_list[jnp.minimum(start + n, outer - 1)] for n in range(height)]

            def step(start_inner, depth, total):
                cols = [inner_list[start_inner + n] for n in range(depth)]
                left = jnp.concatenate(
                    [
                        jnp.concatenate(
                            [left_ref[block_at(i), block_at(j)] for j in cols], axis=1
                        )
                        for i in rows
                    ],
                    axis=0,
                )
                high, low = halves(left)
                right = jnp.concatenate(
                    [split[inner_place[start_inner + n]] for n in range(depth)], axis=0
                )
                wide = jnp.dot(high, right, preferred_element_type=jnp.float32)
                narrow = jnp.dot(low, right[:, :BLOCK_SIDE], preferred_element_type=jnp.float32)
                return total + (wide[:, :BLOCK_SIDE] + (wide[:, BLOCK_SIDE:] + narrow))

            total = jnp.zeros((height * BLOCK_SIDE, BLOCK_SIDE), jnp.float32)
            total = lax.fori_loop(0, inner_fours, lambda n, t: step(4 * n, 4, t), total)
            total = lax.fori_loop(0, inner_twos, lambda n, t: step(4 * inner_fours, 2, t), total)
            for n, i in enumerate(rows):
                out_ref[slot_ref[i * columns + column]] = total[
                    n * BLOCK_SIDE : (n + 1) * BLOCK_SIDE
                ]

        inner_fours, inner_twos = fours_and_twos(inner)
        outer_fours, outer_twos = fours_and_twos(outer)

        @pl.loop(0, outer_fours)
        def _(group):
            outer_group(4 * group, 4)

        @pl.loop(0, outer_twos)
        def _(group):
            outer_group(4 * outer_fours, 2)


def multiply_tiles(place, slot, left, plane, count):
    col_blocks, columns = place.shape
    row_blocks = slot.shape[0]
    tiles = plane.shape[0]
    return pl.pallas_call(
        functools.partial(multiply_kernel, row_blocks, col_blocks, columns, tiles),
        out_shape=jax.ShapeDtypeStruct((count, BLOCK_SIDE, BLOCK_SIDE), jnp.float32),
        in_specs=[SMEM_SPEC, SMEM_SPEC, pl.BlockSpec(memory_space=pl.ANY), VMEM_SPEC],
        out_specs=VMEM_SPEC,
        scratch_shapes=[
            pltpu.VMEM(left.shape, jnp.float32),
            pltpu.SemaphoreType.DMA,
            pltpu.VMEM((tiles + 1, BLOCK_SIDE, 2 * BLOCK_SIDE), jnp.bfloat16),
            pltpu.SMEM((col_blocks + 4,), jnp.int32),
            pltpu.SMEM((col_blocks + 4,), jnp.int32),
            pltpu.SMEM((row_blocks + 2,), jnp.int32),
        ],
        compiler_params=pltpu.CompilerParams(vmem_limit_bytes=VMEM_LIMIT),
        name="multiply_tiles",
    )(place.reshape(-1), slot.reshape(-1), left, plane)


def finish_kernel(
    ranks_row,
    ranks_col,
    cuts,
    capacity_one,
    sizes,
    rank_ref,
    parent_place_ref,
    parent_block_ref,
    parts_ref,
    one_ref,
    two_ref,
    link_ref,
    diag_one_ref,
    diag_two_ref,
    off_one_ref,
    off_two_ref,
    final_ref,
    near,
    both,
    far,
    level_one,
    summed,
    inner_own,
    all_one,
    all_inner,
    dense,
    solved,
    parent,
    sums,
    reduced,
    *sems,
):
    near_send, near_recv, far_send, far_recv = sems[:4]
    one_send, one_recv, inner_send, inner_recv = sems[4:8]
    fold_send, fold_recv, last_send, last_recv = sems[8:]
    row_blocks, blocks_one, blocks_two = sizes
    blocks = blocks_one + blocks_two
    groups = ranks_col // 2
    owners = last_recv.shape[0]
    row, col = lax.axis_index("row"), lax.axis_index("col")
    group, parity = lax.div(col, 2), lax.rem(col, 2)
    sibling = 2 * group + 1 - parity
    others = [lax.rem(group + step, groups) for step in range(1, groups)]
    pieces = range(len(cuts))

    barrier = pltpu.get_barrier_semaphore()
    pl.semaphore_signal(barrier, inc=1, device_id={"col": sibling}, device_id_type=MESH)
    for other in others:
        pl.semaphore_signal(
            barrier, inc=1, device_id={"col": 2 * other + parity}, device_id_type=MESH
        )

    @pl.loop(1, ranks_row)
    def _(step):
        pl.semaphore_signal(
            barrier,
            inc=1,
            device_id={"row": lax.rem(row + step, ranks_row)},
            device_id_type=MESH,
        )

    pl.semaphore_wait(barrier, groups + ranks_row - 1)

    def remote(source, target, send, recv, device):
        return pltpu.make_async_remote_copy(
            src_ref=source,
            dst_ref=target,
            send_sem=send,
            recv_sem=recv,
            device_id=device,
            device_id_type=MESH,
        )

    def to_sibling(to_group, piece):
        return remote(
            parts_ref.at[2 * to_group + 1 - parity, cuts[piece]],
            near.at[to_group, cuts[piece]],
            near_send.at[to_group, piece],
            near_recv.at[to_group, piece],
            {"col": sibling},
        )

    def to_group(other, piece):
        return remote(
            both.at[other, cuts[piece]],
            far.at[group, cuts[piece]],
            far_send.at[other, piece],
            far_recv.at[group, piece],
            {"col": 2 * other + parity},
        )

    def from_group(other, piece):
        return remote(
            both.at[other, cuts[piece]],
            far.at[other, cuts[piece]],
            far_send.at[other, piece],
            far_recv.at[other, piece],
            {"col": 2 * other + parity},
        )

    for piece in pieces:
        for other in others + [group]:
            to_sibling(other, piece).start()
    for piece in pieces:
        for other in others:
            to_sibling(other, piece).wait_recv()

            @pl.loop(cuts[piece].start, cuts[piece].start + cuts[piece].size)
            def _(tile):
                both[other, tile] = parts_ref[2 * other + parity, tile] + near[other, tile]

            to_group(other, piece).start()

    def total_of(piece, target):
        to_sibling(group, piece).wait_recv()
        for other in others:
            from_group(other, piece).wait_recv()

        @pl.loop(cuts[piece].start, cuts[piece].start + cuts[piece].size)
        def _(tile):
            total = parts_ref[col, tile] + near[group, tile]
            for other in others:
                total = total + far[other, tile]
            target[tile] = total

    def spread_one(source, target, send, recv):
        copies = [remote(source, target.at[col], send.at[0], recv.at[col], {"col": sibling})]
        for number, other in enumerate(others):
            copies.append(
                remote(
                    source,
                    target.at[col],
                    send.at[1 + number],
                    recv.at[col],
                    {"col": 2 * other + parity},
                )
            )
        return copies

    total_of(0, level_one)
    one_copies = spread_one(level_one, all_one, one_send, one_recv)
    for copy in one_copies:
        copy.start()

    chunk = min(row_blocks, 4)
    for k in range(blocks_one):
        cols = pl.ds(k * BLOCK_SIDE, BLOCK_SIDE)

        @pl.loop(0, row_blocks)
        def _(block):
            rank = rank_ref[block * blocks + k]
            tile = jnp.where(rank >= 0, level_one[jnp.maximum(rank, 0)], 0.0)
            dense[block_at(block)] = tile
            off_one_ref[block_at(block), cols] = -tile

        first_row = (row == 0).astype(jnp.float32)
        inner_own[k] = first_row * diag_one_ref[:, cols]

        @pl.loop(0, row_blocks // chunk)
        def _(part):
            rows = pl.ds(
                pl.multiple_of(part * (chunk * BLOCK_SIDE), BLOCK_SIDE), chunk * BLOCK_SIDE
            )
            inner_own[k] += dot_f32(one_ref[rows, cols], dense[rows], TRANSPOSED)

    inner_copies = spread_one(inner_own, all_inner, inner_send, inner_recv)
    for copy in inner_copies:
        copy.start()

    for piece in pieces[1:]:
        total_of(piece, summed)

    forwards = []
    for source, target, send, recv in (
        (level_one, all_one, one_send, one_recv),
        (inner_own, all_inner, inner_send, inner_recv),
    ):
        for number, other in enumerate(others):
            origin = 2 * other + parity
            remote(source, target.at[origin], send.at[0], recv.at[origin], {"col": sibling}).wait_recv()
            forward = remote(
                target.at[origin],
                target.at[origin],
                send.at[groups + number],
                recv.at[origin],
                {"col": sibling},
            )
            forward.start()
            forwards.append(forward)
    for source, target, send, recv in (
        (level_one, all_one, one_send, one_recv),
        (inner_own, all_inner, inner_send, inner_recv),
    ):
        for other in others + [group]:
            origin = 2 * other + 1 - parity
            remote(source, target.at[origin], send.at[0], recv.at[origin], {"col": sibling}).wait_recv()

    @pl.loop(0, capacity_one)
    def _(tile):
        all_one[col, tile] = level_one[tile]
        summed[tile] = level_one[tile]

    for k in range(blocks_one):
        all_inner[col, k] = inner_own[k]

    for m in range(blocks_two):
        cols = pl.ds(m * BLOCK_SIDE, BLOCK_SIDE)
        link = link_ref[:, cols]
        across_cols = cols
        diag_cols = pl.ds((blocks_two + m) * BLOCK_SIDE, BLOCK_SIDE)
        sums[:, across_cols] = jnp.zeros((BLOCK_SIDE, BLOCK_SIDE), jnp.float32)
        sums[:, diag_cols] = (row == 0).astype(jnp.float32) * diag_two_ref[:, cols]

        @pl.loop(0, row_blocks)
        def _(block):
            rank = rank_ref[block * blocks + blocks_one + m]
            place = parent_place_ref[block * blocks_two + m]
            keep = rank >= 0
            rows = block_at(block)
            tile = all_one[lax.div(place, capacity_one), lax.rem(place, capacity_one)]
            parent[rows] = jnp.where(keep, tile, 0.0)
            solved[rows] = jnp.where(keep, summed[jnp.maximum(rank, 0)], 0.0)
            dense[rows] = jnp.where(keep, two_ref[rows, cols], 0.0)

        @pl.loop(0, row_blocks // chunk)
        def _(part):
            rows = pl.ds(
                pl.multiple_of(part * (chunk * BLOCK_SIDE), BLOCK_SIDE), chunk * BLOCK_SIDE
            )
            above = parent[rows]
            here = solved[rows] - dot_f32(above, link, PLAIN)
            off_two_ref[rows, cols] = -here
            factor = dense[rows]
            sums[:, diag_cols] += dot_f32(factor, here, TRANSPOSED)
            sums[:, across_cols] -= dot_f32(above, factor, TRANSPOSED)

        block = parent_block_ref[m]
        across = sums[:, across_cols] + dot_f32(
            all_inner[lax.div(block, blocks_one), lax.rem(block, blocks_one)], link, PLAIN
        )
        sums[:, across_cols] = across
        sums[:, diag_cols] += dot_f32(link, across, TRANSPOSED)
    for k in range(blocks_one):
        sums[:, pl.ds((2 * blocks_two + k) * BLOCK_SIDE, BLOCK_SIDE)] = inner_own[k]

    height = BLOCK_SIDE // owners

    def band(owner):
        return pl.ds(pl.multiple_of(owner * height, height), height)

    def fold(owner, origin):
        return remote(
            sums.at[band(owner)],
            reduced.at[origin],
            fold_send.at[owner],
            fold_recv.at[origin],
            {"row": owner},
        )

    @pl.loop(0, owners)
    def _(owner):
        @pl.when(owner != row)
        def _():
            fold(owner, row).start()

    @pl.when(row < owners)
    def _():
        @pl.loop(1, ranks_row)
        def _(step):
            origin = lax.rem(row + step, ranks_row)
            remote(
                sums.at[band(row)],
                reduced.at[origin],
                fold_send.at[0],
                fold_recv.at[origin],
                {"row": origin},
            ).wait_recv()

        reduced[row] = sums[band(row)]
        final_ref[band(row)] = reduced[0]

        @pl.loop(1, ranks_row)
        def _(origin):
            final_ref[band(row)] += reduced[origin]

        @pl.loop(1, ranks_row)
        def _(step):
            target = lax.rem(row + step, ranks_row)
            remote(
                final_ref.at[band(row)],
                final_ref.at[band(row)],
                last_send.at[target],
                last_recv.at[row],
                {"row": target},
            ).start()

    @pl.loop(0, owners)
    def _(owner):
        @pl.when(owner != row)
        def _():
            fold(owner, row).wait_send()
            remote(
                final_ref.at[band(owner)],
                final_ref.at[band(owner)],
                last_send.at[0],
                last_recv.at[owner],
                {"row": owner},
            ).wait_recv()

    @pl.when(row < owners)
    def _():
        @pl.loop(1, ranks_row)
        def _(step):
            target = lax.rem(row + step, ranks_row)
            remote(
                final_ref.at[band(row)],
                final_ref.at[band(row)],
                last_send.at[target],
                last_recv.at[row],
                {"row": target},
            ).wait_send()

    for piece in pieces:
        for other in others + [group]:
            to_sibling(other, piece).wait_send()
        for other in others:
            to_group(other, piece).wait_send()
    for copy in one_copies + inner_copies + forwards:
        copy.wait_send()


def finish(
    rank, parent_place, parent_block, parts, one, two, link, diag_one, diag_two, levels, collective
):
    ranks_row, ranks_col = lax.axis_size("row"), lax.axis_size("col")
    capacity, capacity_one = levels
    row_blocks, blocks = rank.shape
    blocks_one, blocks_two = one.shape[1] // BLOCK_SIDE, two.shape[1] // BLOCK_SIDE
    groups = ranks_col // 2
    owners = min(ranks_row, BLOCK_SIDE // 8)
    middle = (capacity_one + capacity + 1) // 2
    edges = [0, capacity_one, middle, capacity]
    if middle >= capacity:
        edges = [0, capacity_one, capacity]
    cuts = [pl.ds(low, high - low) for low, high in zip(edges[:-1], edges[1:])]
    width = (2 * blocks_two + blocks_one) * BLOCK_SIDE
    tile = (BLOCK_SIDE, BLOCK_SIDE)
    by_piece = pltpu.SemaphoreType.DMA((groups, len(cuts)))
    by_copy = pltpu.SemaphoreType.DMA((2 * groups,))
    by_col = pltpu.SemaphoreType.DMA((ranks_col,))
    by_row = pltpu.SemaphoreType.DMA((ranks_row,))
    by_owner = pltpu.SemaphoreType.DMA((owners,))
    return pl.pallas_call(
        functools.partial(
            finish_kernel,
            ranks_row,
            ranks_col,
            cuts,
            capacity_one,
            (row_blocks, blocks_one, blocks_two),
        ),
        out_shape=(
            jax.ShapeDtypeStruct(one.shape, jnp.float32),
            jax.ShapeDtypeStruct(two.shape, jnp.float32),
            jax.ShapeDtypeStruct((BLOCK_SIDE, width), jnp.float32),
        ),
        in_specs=[SMEM_SPEC] * 3 + [VMEM_SPEC] * 6,
        out_specs=(VMEM_SPEC,) * 3,
        scratch_shapes=[
            pltpu.VMEM((groups, capacity) + tile, jnp.float32),
            pltpu.VMEM((groups, capacity) + tile, jnp.float32),
            pltpu.VMEM((groups, capacity) + tile, jnp.float32),
            pltpu.VMEM((capacity_one,) + tile, jnp.float32),
            pltpu.VMEM((capacity,) + tile, jnp.float32),
            pltpu.VMEM((blocks_one,) + tile, jnp.float32),
            pltpu.VMEM((ranks_col, capacity_one) + tile, jnp.float32),
            pltpu.VMEM((ranks_col, blocks_one) + tile, jnp.float32),
            pltpu.VMEM((row_blocks * BLOCK_SIDE, BLOCK_SIDE), jnp.float32),
            pltpu.VMEM((row_blocks * BLOCK_SIDE, BLOCK_SIDE), jnp.float32),
            pltpu.VMEM((row_blocks * BLOCK_SIDE, BLOCK_SIDE), jnp.float32),
            pltpu.VMEM((BLOCK_SIDE, width), jnp.float32),
            pltpu.VMEM((ranks_row, BLOCK_SIDE // owners, width), jnp.float32),
            by_piece,
            by_piece,
            by_piece,
            by_piece,
            by_copy,
            by_col,
            by_copy,
            by_col,
            by_owner,
            by_row,
            by_row,
            by_owner,
        ],
        compiler_params=pltpu.CompilerParams(
            collective_id=collective, has_side_effects=True, vmem_limit_bytes=VMEM_LIMIT
        ),
        name="finish",
    )(
        rank.reshape(-1),
        parent_place.reshape(-1),
        parent_block,
        parts.reshape((ranks_col, capacity) + tile),
        one,
        two,
        link,
        diag_one,
        diag_two,
    )


def capacity_levels(total, total_one):
    full = (total, total_one)
    if total < 16:
        return (full,)
    parts = ((22, 33), (24, 35), (26, 37), (28, 40), (31, 42), (36, 45))
    return tuple((-(-total * p // 48), -(-total_one * q // 48)) for p, q in parts) + (full,)


def with_capacity(
    collective,
    levels,
    tables,
    root_inverse,
    lower_one,
    diag_one,
    lower_two,
    parent_two,
    lower_parent,
    diag_two,
):
    order, rank = tables
    capacity, capacity_one = levels
    ranks_row, ranks_col, total = rank.shape
    row, col = lax.axis_index("row"), lax.axis_index("col")
    rows_here, cols_here = root_inverse.shape
    row_blocks = rows_here // BLOCK_SIDE
    col_one, col_two = (
        lower_one.shape[1] // BLOCK_SIDE,
        lower_two.shape[1] // BLOCK_SIDE,
    )
    blocks = col_one + col_two
    share = ranks_row // ranks_col

    plane = gather_plane(pack_pair(order[:capacity], lower_one, lower_two), 2 * collective)

    here = lax.dynamic_slice_in_dim(rank, col * share, share, 0)
    base = (
        jnp.arange(ranks_col, dtype=jnp.int32)[None, :, None] * share
        + jnp.arange(share, dtype=jnp.int32)[:, None, None]
    ) * capacity
    place = jnp.where(here >= 0, here + base, -1).reshape(share, ranks_col, row_blocks, blocks)
    place = place.transpose(0, 2, 1, 3).reshape(share * row_blocks, ranks_col * blocks)
    mine = lax.dynamic_index_in_dim(rank, row, 0, False)
    start = jnp.arange(ranks_col, dtype=jnp.int32)[:, None] * capacity
    slot = jnp.where(mine >= 0, mine + start, -1).reshape(ranks_col, row_blocks, blocks)
    slot = slot.transpose(1, 0, 2).reshape(row_blocks, ranks_col * blocks)
    partial_sum = multiply_tiles(
        place,
        slot,
        root_inverse,
        plane.reshape(-1, BLOCK_SIDE, BLOCK_SIDE),
        ranks_col * capacity,
    )
    own_rank = lax.dynamic_index_in_dim(mine, col, 0, False).reshape(row_blocks, blocks)
    parents = lax.dynamic_slice_in_dim(parent_two, col * col_two, col_two, 0)
    first = mine.reshape(ranks_col, row_blocks, blocks)[:, :, :col_one]
    first = first + jnp.arange(ranks_col, dtype=jnp.int32)[:, None, None] * capacity_one
    first = first.transpose(1, 0, 2).reshape(row_blocks, ranks_col * col_one)
    parent_place = jnp.where(own_rank[:, col_one:] >= 0, jnp.take(first, parents, axis=1), 0)
    inverse_off_one, inverse_off_two, final = finish(
        own_rank,
        parent_place,
        parents,
        partial_sum,
        lower_one,
        lower_two,
        lower_parent,
        diag_one,
        diag_two,
        levels,
        2 * collective + 1,
    )
    width = col_two * BLOCK_SIDE
    return (
        inverse_off_one,
        final[:, 2 * width :],
        inverse_off_two,
        -final[:, :width],
        final[:, width : 2 * width],
    )


def local(
    root_inverse,
    lower_one,
    pattern_one,
    diag_one,
    lower_two,
    pattern_two,
    parent_two,
    lower_parent,
    diag_two,
):
    ranks_row, ranks_col = lax.axis_size("row"), lax.axis_size("col")
    row_blocks = root_inverse.shape[0] // BLOCK_SIDE
    pattern = jnp.concatenate(
        [
            pattern_one.reshape(ranks_row, row_blocks, ranks_col, -1),
            pattern_two.reshape(ranks_row, row_blocks, ranks_col, -1),
        ],
        axis=3,
    )
    pattern = pattern.transpose(0, 2, 1, 3).reshape(ranks_row, ranks_col, -1).astype(jnp.int32)
    total = pattern.shape[2]
    blocks_one = pattern_one.shape[1] // ranks_col
    tile = np.arange(total)
    blocks = total // row_blocks
    turn = tile + total * (tile % blocks >= blocks_one)
    ahead = jnp.asarray(turn[:, None] <= turn[None, :], jnp.float32)
    running = jnp.dot(pattern.astype(jnp.float32), ahead, precision=lax.Precision.HIGHEST)
    running = running.astype(jnp.int32)
    rank = jnp.where(pattern > 0, running - 1, -1)
    first = jnp.asarray(tile % blocks < blocks_one)
    counts = jnp.max(rank, axis=2) + 1
    counts_one = jnp.max(jnp.where(first, rank, -1), axis=2) + 1
    own = lax.dynamic_index_in_dim(rank, lax.axis_index("row"), 0, False)
    own = lax.dynamic_index_in_dim(own, lax.axis_index("col"), 0, False)
    order = jnp.sum(
        jnp.where(own[None, :] == tile[:, None].astype(np.int32), tile.astype(np.int32), 0),
        axis=1,
        dtype=jnp.int32,
    )
    levels = capacity_levels(total, row_blocks * blocks_one)
    operands = (
        (order, rank),
        root_inverse,
        lower_one,
        diag_one,
        lower_two,
        parent_two,
        lower_parent,
        diag_two,
    )
    branches = [
        functools.partial(with_capacity, number, level) for number, level in enumerate(levels)
    ]
    if len(branches) == 1:
        return branches[0](*operands)
    peak = jnp.stack([jnp.max(counts), jnp.max(counts_one)])
    over = jnp.any(peak > jnp.array(levels[:-1], dtype=jnp.int32), axis=1)
    index = jnp.sum(over).astype(jnp.int32)
    return lax.switch(index, branches, *operands)


def solution(mesh):
    return jax.shard_map(
        local,
        mesh=mesh,
        in_specs=(
            P(("pole", "row"), "col"),
            P(("pole", "row"), "col"),
            P(),
            P("pole", "col"),
            P(("pole", "row"), "col"),
            P(),
            P(),
            P("pole", "col"),
            P("pole", "col"),
        ),
        out_specs=(
            P(("pole", "row"), "col"),
            P("pole", "col"),
            P(("pole", "row"), "col"),
            P("pole", "col"),
            P("pole", "col"),
        ),
        check_vma=False,
    )
```
